256 devices in a mesh: seq: 8 (over y, x_hi), dp: 32 (over z, x_lo, core).
Axes of the slice: x: 4 (x_hi: 2, x_lo: 2; x = x_hi * 2 + x_lo), y: 4, z: 8, core: 2. Of those that a mesh axis runs over, the one named last changes fastest.
Arguments:
- layer_input: bfloat16 [32, 2048, 8192], P('dp', 'seq'), may hold values from -400 to 400
- frozen_queries: bfloat16 [32, 2048, 6144], P('dp', 'seq'), may hold values from -70 to 70
- frozen_keys: bfloat16 [32, 2048, 768], P('dp', 'seq'), may hold values from -6 to 6
- frozen_values: bfloat16 [32, 2048, 768], P('dp', 'seq'), may hold values from -6 to 6
- output_gradient: bfloat16 [32, 2048, 6144], P('dp', 'seq'), may hold values from -6 to 6
- norm_scale_vector: bfloat16 [8192], replicated, may hold values from 0.5 to 1.5
- query_down_weight: bfloat16 [8, 8192], replicated, may hold values from -0.0625 to 0.0625
- query_up_weight: bfloat16 [8, 6144], replicated, may hold values from -2 to 2
- value_down_weight: bfloat16 [8, 8192], replicated, may hold values from -0.0625 to 0.0625
- value_up_weight: bfloat16 [8, 768], replicated, may hold values from -2 to 2
- head_ordering: int32 [6], replicated, may hold values from 0 to 5, each once
Outputs:
- grad_query_a: float32 [8, 8192], replicated
- grad_query_b: float32 [8, 6144], replicated
- grad_value_a: float32 [8, 8192], replicated
- grad_value_b: float32 [8, 768], replicated
- grad_gain: float32 [8192], replicated
The draws below stay inside these ranges and needn't reach their ends.
Inputs may be any that keep to these rules, and one draw needn't show every extreme that they name: `head_ordering`: a permutation of the 6 key-value heads.
All inputs are finite; a program needn't handle non-finite values.
Results may differ from the reference program's by a relative error of at most 0.012.
The reference program's roundings to bfloat16 on the way count: a program that leaves them out, or rounds other values in their place, can miss the bound.
Values may be sent and summed in bfloat16 or wider, within the bound.
No kernel may reach another device: no remote copies, remote signals or barrier semaphores. Data moves between devices by JAX's collectives and lax.ppermute only.
A program may use at most 128 MiB of HBM per device.

```python
import math
from functools import partial
import jax
import jax.numpy as jnp
from jax import lax

MODEL_WIDTH = 8192
HEAD_SIZE = 128
QUERY_HEADS = 48
KEY_VALUE_HEADS = 6
ADAPTER_RANK = 8
G = 512
SEQUENCE_LENGTH = 2048
BATCH_COUNT = 32


def drawn_pair(key):
    query_layout = (BATCH_COUNT, SEQUENCE_LENGTH, KEY_VALUE_HEADS, QUERY_HEADS // KEY_VALUE_HEADS, HEAD_SIZE)
    key_layout = (BATCH_COUNT, SEQUENCE_LENGTH, KEY_VALUE_HEADS, HEAD_SIZE)
    key_rows = jax.random.truncated_normal(jax.random.fold_in(key, 102), -6.0, 6.0, key_layout, jnp.float32)
    queries = jax.random.truncated_normal(jax.random.fold_in(key, 103), -6.0, 6.0, query_layout, jnp.float32)
    return (queries, key_rows)


def draw_frozen_queries(key, part):
    queries, key_rows = drawn_pair(key)
    return queries.reshape(BATCH_COUNT, SEQUENCE_LENGTH, QUERY_HEADS * HEAD_SIZE).astype(jnp.bfloat16)


def draw_frozen_keys(key, part):
    queries, key_rows = drawn_pair(key)
    return key_rows.reshape(BATCH_COUNT, SEQUENCE_LENGTH, KEY_VALUE_HEADS * HEAD_SIZE).astype(jnp.bfloat16)


def draw_layer_input(key, part):
    row_scale = jnp.exp(jax.random.uniform(jax.random.fold_in(key, 201), (BATCH_COUNT, SEQUENCE_LENGTH, 1), jnp.float32, 0.0, math.log(10.0)))
    col_scale = jnp.exp(jax.random.uniform(jax.random.fold_in(key, 202), (1, 1, MODEL_WIDTH), jnp.float32, 0.0, math.log(10.0)))
    base = jax.random.truncated_normal(jax.random.fold_in(key, 203), -4.0, 4.0, (BATCH_COUNT, SEQUENCE_LENGTH, MODEL_WIDTH), jnp.float32)
    return (base * row_scale * col_scale).astype(jnp.bfloat16)


def block_scale(key, shape, shards, low, high):
    factor_of = 1.0
    for dim, shards_of in shards:
        heights = jax.random.uniform(jax.random.fold_in(jax.random.fold_in(key, 6), dim), (shards_of,), jnp.float32, low / len(shards), high / len(shards))
        factor_of = factor_of * jnp.repeat(jnp.exp(heights), shape[dim] // shards_of).reshape((-1,) + (1,) * (len(shape) - 1 - dim))
    return factor_of


def normal_values(stream_key, shape, deviation, reach, cuts=(), kind=jnp.bfloat16):
    loudness = block_scale(stream_key, shape, cuts, -0.22, 0.18) if cuts else 1.0
    values = jax.random.normal(stream_key, shape, jnp.float32) * deviation * loudness
    return jnp.minimum(jnp.maximum(values, -reach), reach).astype(kind)


def setup_inputs(seed: int = 0) -> dict:
    arg_keys = jax.random.split(jax.random.key(seed), 12)
    layer_input = draw_layer_input(jax.random.fold_in(arg_keys[11], 71), 0)
    frozen_queries = draw_frozen_queries(jax.random.fold_in(arg_keys[11], 71), 0)
    frozen_keys = draw_frozen_keys(jax.random.fold_in(arg_keys[11], 71), 0)
    frozen_values = normal_values(arg_keys[3], (BATCH_COUNT, SEQUENCE_LENGTH, KEY_VALUE_HEADS * HEAD_SIZE), 1.0, 6.0, ((0, 32), (1, 8)))
    output_gradient = normal_values(arg_keys[4], (BATCH_COUNT, SEQUENCE_LENGTH, QUERY_HEADS * HEAD_SIZE), 1.0, 6.0, ((0, 32), (1, 8)))
    norm_scale_vector = jnp.clip(jax.random.uniform(arg_keys[5], (MODEL_WIDTH,), jnp.float32, 0.5, 1.5), 0.5, 1.5).astype(jnp.bfloat16)
    query_down_weight = normal_values(arg_keys[6], (ADAPTER_RANK, MODEL_WIDTH), MODEL_WIDTH ** -0.5, 0.0625)
    query_up_weight = normal_values(arg_keys[7], (ADAPTER_RANK, QUERY_HEADS * HEAD_SIZE), ADAPTER_RANK ** -0.5, 2.0)
    value_down_weight = normal_values(arg_keys[8], (ADAPTER_RANK, MODEL_WIDTH), MODEL_WIDTH ** -0.5, 0.0625)
    value_up_weight = normal_values(arg_keys[9], (ADAPTER_RANK, KEY_VALUE_HEADS * HEAD_SIZE), ADAPTER_RANK ** -0.5, 2.0)
    head_ordering = jax.random.permutation(arg_keys[10], KEY_VALUE_HEADS).astype(jnp.int32)
    return dict(layer_input=layer_input, frozen_queries=frozen_queries, frozen_keys=frozen_keys, frozen_values=frozen_values, output_gradient=output_gradient, norm_scale_vector=norm_scale_vector, query_down_weight=query_down_weight, query_up_weight=query_up_weight, value_down_weight=value_down_weight, value_up_weight=value_up_weight, head_ordering=head_ordering)


EPS = 1e-05
ADAPTER_SCALE = 2.0

def attend_group(query_rows, key_rows, values, grad_out, allowed):
    factor = 1.0 / math.sqrt(HEAD_SIZE)
    keys_f = key_rows.astype(jnp.float32)
    values_f = values.astype(jnp.float32)
    grads_f = grad_out.astype(jnp.float32)
    scores = jnp.einsum('tgd,ud->gtu', query_rows.astype(jnp.float32), keys_f) * factor
    scores = jnp.where(allowed[None], scores, -jnp.inf)
    row_max = lax.optimization_barrier(jnp.max(scores, axis=-1, keepdims=True))
    exponent = jnp.exp(scores - row_max)
    probs_full = exponent / lax.optimization_barrier(jnp.sum(exponent, axis=-1, keepdims=True))
    weights = lax.optimization_barrier(probs_full.astype(jnp.bfloat16)).astype(jnp.float32)
    attended = jnp.einsum('gtu,ud->tgd', weights, values_f)
    delta = lax.optimization_barrier(jnp.sum(grads_f * attended, axis=-1))
    dprob = jnp.einsum('tgd,ud->gtu', grads_f, values_f)
    dscore = probs_full * (dprob - delta.T[:, :, None])
    dscore_b = lax.optimization_barrier(dscore.astype(jnp.bfloat16)).astype(jnp.float32)
    query_gradient = jnp.einsum('gtu,ud->tgd', dscore_b, keys_f) * factor
    value_gradient = jnp.einsum('gtu,tgd->ud', weights, grads_f)
    return (query_gradient, value_gradient)

def head_grads(operands):
    query_h, keys_h, values_h, grads_h, offset = operands

    def regroup(array):
        rolled_array = jnp.roll(array, -offset, axis=0)
        return rolled_array.reshape((SEQUENCE_LENGTH // G, G) + array.shape[1:])
    positions = jnp.arange(G)
    causal = positions[None, :] <= positions[:, None]
    query_gradient, value_gradient = jax.vmap(partial(attend_group, allowed=causal))(regroup(query_h), regroup(keys_h), regroup(values_h), regroup(grads_h))
    query_gradient = jnp.roll(query_gradient.reshape(query_h.shape), offset, axis=0)
    value_gradient = jnp.roll(value_gradient.reshape(keys_h.shape), offset, axis=0)
    return (query_gradient.astype(jnp.bfloat16), value_gradient.astype(jnp.bfloat16))

def reference(layer_input, frozen_queries, frozen_keys, frozen_values, output_gradient, norm_scale_vector, query_down_weight, query_up_weight, value_down_weight, value_up_weight, head_ordering):
    displaced_index = head_ordering[:KEY_VALUE_HEADS // 2]
    displaced_mask = jnp.any(displaced_index[:, None] == jnp.arange(KEY_VALUE_HEADS, dtype=jnp.int32)[None, :], axis=0)
    shift_amounts = jnp.where(displaced_mask, G // 2, 0).astype(jnp.int32)

    def one_sequence(totals, operands):
        hidden_s, query_slices, key_slices, value_slices, gradient_slices = operands
        hidden_f = hidden_s.astype(jnp.float32)
        inverse = lax.rsqrt(lax.optimization_barrier(jnp.mean(hidden_f * hidden_f, axis=-1, keepdims=True)) + EPS)
        unit = hidden_f * inverse
        normalized_input = (unit * norm_scale_vector.astype(jnp.float32)).astype(jnp.bfloat16)
        query_inner = jnp.dot(normalized_input, query_down_weight.T, preferred_element_type=jnp.float32).astype(jnp.bfloat16)
        value_inner = jnp.dot(normalized_input, value_down_weight.T, preferred_element_type=jnp.float32).astype(jnp.bfloat16)
        query_rows = (query_slices.astype(jnp.float32) + ADAPTER_SCALE * jnp.dot(query_inner, query_up_weight, preferred_element_type=jnp.float32)).astype(jnp.bfloat16)
        value_rows = (value_slices.astype(jnp.float32) + ADAPTER_SCALE * jnp.dot(value_inner, value_up_weight, preferred_element_type=jnp.float32)).astype(jnp.bfloat16)
        head_wise = (jnp.moveaxis(query_rows.reshape(SEQUENCE_LENGTH, KEY_VALUE_HEADS, QUERY_HEADS // KEY_VALUE_HEADS, HEAD_SIZE), 1, 0), jnp.moveaxis(key_slices.reshape(SEQUENCE_LENGTH, KEY_VALUE_HEADS, HEAD_SIZE), 1, 0), jnp.moveaxis(value_rows.reshape(SEQUENCE_LENGTH, KEY_VALUE_HEADS, HEAD_SIZE), 1, 0), jnp.moveaxis(gradient_slices.reshape(SEQUENCE_LENGTH, KEY_VALUE_HEADS, QUERY_HEADS // KEY_VALUE_HEADS, HEAD_SIZE), 1, 0), shift_amounts)
        query_gradient, value_gradient = lax.map(head_grads, head_wise)
        query_gradient = jnp.moveaxis(query_gradient, 0, 1).reshape(SEQUENCE_LENGTH, QUERY_HEADS * HEAD_SIZE)
        value_gradient = jnp.moveaxis(value_gradient, 0, 1).reshape(SEQUENCE_LENGTH, KEY_VALUE_HEADS * HEAD_SIZE)
        query_up_unscaled = ADAPTER_SCALE * jnp.dot(query_inner.T, query_gradient, preferred_element_type=jnp.float32)
        value_up_unscaled = ADAPTER_SCALE * jnp.dot(value_inner.T, value_gradient, preferred_element_type=jnp.float32)
        query_gradient_inner = (ADAPTER_SCALE * jnp.dot(query_gradient, query_up_weight.T, preferred_element_type=jnp.float32)).astype(jnp.bfloat16)
        value_gradient_inner = (ADAPTER_SCALE * jnp.dot(value_gradient, value_up_weight.T, preferred_element_type=jnp.float32)).astype(jnp.bfloat16)
        raw_qa = jnp.dot(query_gradient_inner.T, normalized_input, preferred_element_type=jnp.float32)
        raw_va = jnp.dot(value_gradient_inner.T, normalized_input, preferred_element_type=jnp.float32)
        normalized_gradient = jnp.dot(query_gradient_inner, query_down_weight, preferred_element_type=jnp.float32) + jnp.dot(value_gradient_inner, value_down_weight, preferred_element_type=jnp.float32)
        raw_gain = lax.optimization_barrier(jnp.sum(normalized_gradient * unit, axis=0))
        fresh = (raw_qa, query_up_unscaled, raw_va, value_up_unscaled, raw_gain)
        return (tuple((total + term for total, term in zip(totals, fresh))), None)
    start_position = (jnp.zeros((ADAPTER_RANK, MODEL_WIDTH), jnp.float32), jnp.zeros((ADAPTER_RANK, QUERY_HEADS * HEAD_SIZE), jnp.float32), jnp.zeros((ADAPTER_RANK, MODEL_WIDTH), jnp.float32), jnp.zeros((ADAPTER_RANK, KEY_VALUE_HEADS * HEAD_SIZE), jnp.float32), jnp.zeros((MODEL_WIDTH,), jnp.float32))
    totals, unused = lax.scan(one_sequence, start_position, (layer_input, frozen_queries, frozen_keys, frozen_values, output_gradient))
    squares = jnp.zeros((), jnp.float32)
    for part in totals:
        squares = squares + jnp.sum(part * part)
    listed_items = ADAPTER_RANK * (2 * MODEL_WIDTH + QUERY_HEADS * HEAD_SIZE + KEY_VALUE_HEADS * HEAD_SIZE) + MODEL_WIDTH
    factor = jnp.minimum(1.0, math.sqrt(listed_items) / jnp.sqrt(squares))
    return (totals[0] * factor, totals[1] * factor, totals[2] * factor, totals[3] * factor, totals[4] * factor)
```

```python
import functools
import math

import jax
import jax.numpy as jnp
from jax import lax
from jax.experimental import pallas as pl
from jax.experimental.pallas import tpu as pltpu
from jax.sharding import PartitionSpec as P

HEAD_SIZE = 128
TOKENS = 256
HALF = 128
WIDTH = 8192
RANK = 8
KV_HEADS = 6
SHARE = 8
LANES = SHARE * HEAD_SIZE
EPS = 1e-05
FACTOR = 1.0 / math.sqrt(HEAD_SIZE)
LOG2_E = 1.4426950408889634
TILES = 96
QB_TILE = 64
F32 = jnp.float32
BF16 = jnp.bfloat16
BOTH = ("seq", "dp")
MIB = 1024 * 1024


def nn(left, right):
    return jnp.dot(left, right, preferred_element_type=F32)


def nt(left, right):
    return lax.dot_general(left, right, (((1,), (1,)), ((), ())), preferred_element_type=F32)


def norm_kernel(x_ref, scale_ref, down_ref, normed_ref, qm_ref, vm_ref, qmt_ref, vmt_ref):
    step = 1024
    total = jnp.zeros((HALF, HEAD_SIZE), F32)
    for start in range(0, WIDTH, HEAD_SIZE):
        part = x_ref[:, start : start + HEAD_SIZE].astype(F32)
        total = total + part * part
    mean = jnp.sum(total, axis=1, keepdims=True) * (1.0 / WIDTH)
    inverse = lax.rsqrt(mean + EPS)
    mid = jnp.zeros((HALF, 2 * RANK), F32)
    for start in range(0, WIDTH, step):
        cols = slice(start, start + step)
        unit = x_ref[:, cols].astype(F32) * inverse
        normed = (unit * scale_ref[:, cols].astype(F32)).astype(BF16)
        normed_ref[:, cols] = normed
        mid = mid + nt(normed, down_ref[:, cols])
    qm_ref[...] = mid[:, :RANK].astype(BF16)
    vm_ref[...] = mid[:, RANK:].astype(BF16)
    mid_t = mid.T
    qmt_ref[...] = mid_t[:RANK].astype(BF16)
    vmt_ref[...] = mid_t[RANK:].astype(BF16)


def attend_head(prior, q_ref, g_ref, k_ref, v_ref, qm, vm, qup, vup, kp, vp, q_scr, dq_scr):
    keys = k_ref[...]
    keys_t = keys.astype(F32).T.astype(BF16)
    values = (v_ref[...].astype(F32) + 2.0 * nn(vm, vup)).astype(BF16)
    q_scr[...] = (q_ref[...].astype(F32) + 2.0 * nn(qm, qup)).astype(BF16)
    key_id = lax.broadcasted_iota(jnp.int32, (HALF, 2 * HALF), 0)
    query_id = lax.broadcasted_iota(jnp.int32, (HALF, 2 * HALF), 1) % HALF
    allowed = key_id <= query_id
    if prior:
        kp_t = kp.astype(F32).T.astype(BF16)
    dv_low = dv_high = dv_prior = None
    for c in range(2):
        rows = slice(c * HALF, (c + 1) * HALF)
        near = (c + 1) * HALF
        for pair in range(SHARE // 2):
            cols = [slice(g * HEAD_SIZE, (g + 1) * HEAD_SIZE) for g in (2 * pair, 2 * pair + 1)]
            queries = jnp.concatenate([q_scr[rows, cols[0]], q_scr[rows, cols[1]]], axis=0)
            grads = jnp.concatenate([g_ref[rows, cols[0]], g_ref[rows, cols[1]]], axis=0)
            own = nt(keys[:near], queries) * (FACTOR * LOG2_E)
            diagonal = jnp.where(allowed, own[near - HALF :], -jnp.inf)
            parts = [diagonal] if c == 0 else [own[:HALF], diagonal]
            blocks = [(keys_t[:, j * HALF : (j + 1) * HALF], part) for j, part in enumerate(parts)]
            dprob = nt(values[:near], grads)
            dprobs = [dprob[j * HALF : (j + 1) * HALF] for j in range(c + 1)]
            if prior:
                parts.append(nt(kp, queries) * (FACTOR * LOG2_E))
                dprobs.append(nt(vp, grads))
            top = functools.reduce(jnp.maximum, [jnp.max(s, axis=0, keepdims=True) for s in parts])
            exps = [jnp.exp2(s - top) for s in parts]
            denom = functools.reduce(jnp.add, [jnp.sum(e, axis=0, keepdims=True) for e in exps])
            inv = 1.0 / denom
            probs = [e * inv for e in exps]
            weights = [p.astype(BF16) for p in probs]
            delta = functools.reduce(
                jnp.add,
                [jnp.sum(w.astype(F32) * d, axis=0, keepdims=True) for w, d in zip(weights, dprobs)],
            )
            dscore = [(p * (d - delta)).astype(BF16) for p, d in zip(probs, dprobs)]
            if c == 0:
                dq_t = nn(keys_t[:, :HALF], dscore[0])
                own_w = weights[0]
            else:
                dq_t = nn(keys_t, jnp.concatenate(dscore[:2], axis=0))
                own_w = jnp.concatenate(weights[:2], axis=0)
            if prior:
                dq_t = dq_t + nn(kp_t, dscore[-1])
                term = nn(weights[-1], grads)
                dv_prior = term if dv_prior is None else dv_prior + term
            dq_b = (dq_t * FACTOR).astype(BF16)
            dq_scr[cols[0], rows] = dq_b[:, :HALF]
            dq_scr[cols[1], rows] = dq_b[:, HALF:]
            term = nn(own_w, grads)
            dv_low = term[:HALF] if dv_low is None else dv_low + term[:HALF]
            if c == 1:
                dv_high = term[HALF:] if dv_high is None else dv_high + term[HALF:]
    dv = jnp.concatenate([dv_low, dv_high], axis=0).astype(BF16)
    return dv, dv_prior


def add_to(first, ref, value):
    @pl.when(first)
    def _():
        ref[...] = value

    @pl.when(jnp.logical_not(first))
    def _():
        ref[...] = ref[...] + value


def own_kernel(
    ids_ref, q_ref, g_ref, k_ref, v_ref, qm_ref, vm_ref, qmt_ref, vmt_ref, qup_ref, vup_ref,
    qb_ref, vb_ref, dqm_ref, dvm_ref, q_scr, dq_scr,
):
    first = pl.program_id(0) == 0
    qup, vup = qup_ref[...], vup_ref[...]
    dv, _ = attend_head(
        False, q_ref, g_ref, k_ref, v_ref, qm_ref[...], vm_ref[...], qup, vup, None, None, q_scr, dq_scr
    )
    dq_t = dq_scr[...]
    add_to(first, dqm_ref, 2.0 * nn(qup, dq_t))
    add_to(first, dvm_ref, 2.0 * nt(vup, dv))
    qb_ref[0] = 2.0 * nt(qmt_ref[...], dq_t)
    vb_ref[0] = 2.0 * nn(vmt_ref[...], dv)


def prior_kernel(
    ids_ref, q_ref, g_ref, k_ref, v_ref, qm_ref, vm_ref, qmt_ref, vmt_ref, qup_ref, vup_ref,
    kp_ref, vp_ref, vmtp_ref, qb_ref, vb_ref, dqm_ref, dvm_ref, dvp_ref, q_scr, dq_scr,
):
    first = pl.program_id(0) == 0
    qup, vup = qup_ref[...], vup_ref[...]
    vmt_prior = vmtp_ref[...]
    vm_prior = vmt_prior.astype(F32).T.astype(BF16)
    values_prior = (vp_ref[...].astype(F32) + 2.0 * nn(vm_prior, vup)).astype(BF16)
    dv, dv_prior = attend_head(
        True, q_ref, g_ref, k_ref, v_ref, qm_ref[...], vm_ref[...], qup, vup,
        kp_ref[...], values_prior, q_scr, dq_scr,
    )
    dv_prior = dv_prior.astype(BF16)
    dq_t = dq_scr[...]
    add_to(first, dqm_ref, 2.0 * nn(qup, dq_t))
    add_to(first, dvm_ref, 2.0 * nt(vup, dv))
    add_to(first, dvp_ref, 2.0 * nt(vup, dv_prior))
    qb_ref[0] = 2.0 * nt(qmt_ref[...], dq_t)
    vb_ref[0] = 2.0 * nn(vmt_ref[...], dv) + 2.0 * nn(vmt_prior, dv_prior)


def gather_kernel(
    ids_ref, normed_ref, dqm1_ref, dqm2_ref, dvm1_ref, dvm2_ref, dvh_ref,
    qb1_ref, vb1_ref, qb2_ref, vb2_ref, out_ref, buf,
):
    step = pl.program_id(0)

    @pl.when(step < 4)
    def _():
        dq = dqm1_ref[...] + dqm2_ref[...]
        dv = dvm1_ref[...] + dvm2_ref[...] + dvh_ref[...]
        mids = jnp.concatenate([dq, dv], axis=0).astype(BF16)
        for j in range(4):
            part = nn(mids, normed_ref[:, j * 512 : (j + 1) * 512]).astype(BF16)
            for k in range(4):
                out_ref[4 * j + k] = part[:, k * HEAD_SIZE : (k + 1) * HEAD_SIZE]

    @pl.when(step == 4)
    def _():
        buf[27:32] = jnp.zeros((5, 16, HEAD_SIZE), F32)
        for i in range(3):
            for base, qb_ref, vb_ref in ((0, qb2_ref, vb2_ref), (3, qb1_ref, vb1_ref)):
                head = ids_ref[base + i]
                upper = head >= 3
                row = pl.multiple_of(jnp.where(upper, 8, 0), 8)
                place = jnp.where(upper, head - 3, head)
                for k in range(SHARE):
                    buf[place * SHARE + k, pl.ds(row, 8), :] = qb_ref[i][:, k * HEAD_SIZE : (k + 1) * HEAD_SIZE]
                buf[24 + place, pl.ds(row, 8), :] = vb_ref[i]
        for t in range(16):
            out_ref[t] = buf[t].astype(BF16)

    @pl.when(step == 5)
    def _():
        for t in range(16):
            out_ref[t] = buf[16 + t].astype(BF16)


def clip_kernel(limit, sum_ref, qd_ref, vd_ref, scale_ref, qa_ref, qb_ref, va_ref, vb_ref, gain_ref, gains):
    total = jnp.zeros((16, HEAD_SIZE), F32)
    gain_total = jnp.zeros((1, HEAD_SIZE), F32)
    for t in range(QB_TILE):
        cols = slice(t * HEAD_SIZE, (t + 1) * HEAD_SIZE)
        tile = sum_ref[t].astype(F32)
        total = total + tile * tile
        mixed = qd_ref[:, cols].astype(F32) * tile[:RANK] + vd_ref[:, cols].astype(F32) * tile[RANK:]
        gain = jnp.sum(mixed, axis=0, keepdims=True) / scale_ref[:, cols].astype(F32)
        gains[:, cols] = gain
        gain_total = gain_total + gain * gain
    for t in range(QB_TILE, QB_TILE + 27):
        tile = sum_ref[t].astype(F32)
        total = total + tile * tile
    squares = jnp.sum(total, keepdims=True) + jnp.sum(gain_total, keepdims=True)
    factor = jnp.minimum(1.0, limit / jnp.sqrt(squares))
    gain_ref[...] = gains[...] * factor
    for t in range(QB_TILE):
        cols = slice(t * HEAD_SIZE, (t + 1) * HEAD_SIZE)
        tile = sum_ref[t].astype(F32) * factor
        qa_ref[:, cols] = tile[:RANK]
        va_ref[:, cols] = tile[RANK:]
    for t in range(24):
        tile = sum_ref[QB_TILE + t].astype(F32) * factor
        qb_ref[:, t * HEAD_SIZE : (t + 1) * HEAD_SIZE] = tile[:RANK]
        qb_ref[:, (24 + t) * HEAD_SIZE : (25 + t) * HEAD_SIZE] = tile[RANK:]
    for t in range(3):
        tile = sum_ref[QB_TILE + 24 + t].astype(F32) * factor
        vb_ref[:, t * HEAD_SIZE : (t + 1) * HEAD_SIZE] = tile[:RANK]
        vb_ref[:, (3 + t) * HEAD_SIZE : (4 + t) * HEAD_SIZE] = tile[RANK:]


def groups_along(keys):
    found = {}
    for device in range(256):
        y, xh, z, rest = device // 64, device // 32 % 2, device // 4 % 8, device % 4
        place = {"y": y, "xh": xh, "z": z, "xl": rest // 2, "core": rest % 2}
        found.setdefault(tuple(v for k, v in place.items() if k not in keys), []).append(device)
    return list(found.values())


PLANE = groups_along(("y", "xh", "xl", "core"))
COLUMN = groups_along(("z",))


def exchange(array, groups):
    return lax.all_to_all(array, BOTH, 0, 0, tiled=True, axis_index_groups=groups)


def sum_over_devices(tiles):
    shares = tiles.reshape(32, 3, 16, HEAD_SIZE)
    mine = jnp.sum(exchange(shares, PLANE).astype(F32), axis=0)
    copies = jnp.broadcast_to(mine[None], (8, 3, 16, HEAD_SIZE))
    mine = jnp.sum(exchange(copies, COLUMN), axis=0).astype(BF16)
    copies = jnp.broadcast_to(mine[None], (32, 3, 16, HEAD_SIZE))
    return exchange(copies, PLANE).reshape(TILES, 16, HEAD_SIZE)


def from_behind(block, distance):
    return lax.ppermute(block, "seq", [((i - distance) % 8, i) for i in range(8)])


def whole(shape):
    return pl.BlockSpec(shape, lambda *_: (0,) * len(shape))


def params(mib):
    return pltpu.CompilerParams(vmem_limit_bytes=mib * MIB)


def attention_call(prior, base, ids, q, g, k, v, qm, vm, qmt, vmt, qup, vup, extra):
    def by_head(rows, cols):
        return pl.BlockSpec((rows, cols), lambda i, ids: (0, ids[base + i]))

    in_specs = [
        by_head(TOKENS, LANES), by_head(TOKENS, LANES), by_head(TOKENS, HEAD_SIZE), by_head(TOKENS, HEAD_SIZE),
        whole((TOKENS, RANK)), whole((TOKENS, RANK)), whole((RANK, TOKENS)), whole((RANK, TOKENS)),
        by_head(RANK, LANES), by_head(RANK, HEAD_SIZE),
    ]
    if prior:
        in_specs += [by_head(TOKENS, HEAD_SIZE), by_head(TOKENS, HEAD_SIZE), whole((RANK, TOKENS))]
    mids = 3 if prior else 2
    return pl.pallas_call(
        prior_kernel if prior else own_kernel,
        out_shape=[
            jax.ShapeDtypeStruct((3, RANK, LANES), F32),
            jax.ShapeDtypeStruct((3, RANK, HEAD_SIZE), F32),
        ]
        + [jax.ShapeDtypeStruct((RANK, TOKENS), F32)] * mids,
        grid_spec=pltpu.PrefetchScalarGridSpec(
            num_scalar_prefetch=1,
            grid=(3,),
            in_specs=in_specs,
            out_specs=[
                pl.BlockSpec((1, RANK, LANES), lambda i, ids: (i, 0, 0)),
                pl.BlockSpec((1, RANK, HEAD_SIZE), lambda i, ids: (i, 0, 0)),
            ]
            + [whole((RANK, TOKENS))] * mids,
            scratch_shapes=[pltpu.VMEM((TOKENS, LANES), BF16), pltpu.VMEM((LANES, TOKENS), BF16)],
        ),
        compiler_params=params(24),
        cost_estimate=pl.CostEstimate(
            flops=(2 if prior else 1) * 3_000_000_000, bytes_accessed=4_000_000, transcendentals=0
        ),
        name="prior_attention" if prior else "own_attention",
    )(ids, q, g, k, v, qm, vm, qmt, vmt, qup, vup, *extra)


def shards(
    layer_input,
    frozen_queries,
    frozen_keys,
    frozen_values,
    output_gradient,
    norm_scale_vector,
    query_down_weight,
    query_up_weight,
    value_down_weight,
    value_up_weight,
    head_ordering,
):
    x, q, k, v, g = (
        a[0] for a in (layer_input, frozen_queries, frozen_keys, frozen_values, output_gradient)
    )
    keys_prior = from_behind(k, 1)
    values_prior = from_behind(v, 1)
    odd = lax.axis_index("seq") % 2 == 1
    ids = jnp.where(odd, jnp.roll(head_ordering, 3), head_ordering)
    down = jnp.concatenate([query_down_weight, value_down_weight], axis=0)
    scale = norm_scale_vector.reshape(1, WIDTH)

    normed, qm, vm, qmt, vmt = pl.pallas_call(
        norm_kernel,
        out_shape=[
            jax.ShapeDtypeStruct((TOKENS, WIDTH), BF16),
            jax.ShapeDtypeStruct((TOKENS, RANK), BF16),
            jax.ShapeDtypeStruct((TOKENS, RANK), BF16),
            jax.ShapeDtypeStruct((RANK, TOKENS), BF16),
            jax.ShapeDtypeStruct((RANK, TOKENS), BF16),
        ],
        grid=(2,),
        in_specs=[
            pl.BlockSpec((HALF, WIDTH), lambda i: (i, 0)),
            whole((1, WIDTH)),
            whole((2 * RANK, WIDTH)),
        ],
        out_specs=[
            pl.BlockSpec((HALF, WIDTH), lambda i: (i, 0)),
            pl.BlockSpec((HALF, RANK), lambda i: (i, 0)),
            pl.BlockSpec((HALF, RANK), lambda i: (i, 0)),
            pl.BlockSpec((RANK, HALF), lambda i: (0, i)),
            pl.BlockSpec((RANK, HALF), lambda i: (0, i)),
        ],
        compiler_params=params(24),
        name="norm",
    )(x, scale, down)

    vmt_prior = from_behind(vmt, 1)
    shared = (ids, q, g, k, v, qm, vm, qmt, vmt, query_up_weight, value_up_weight)
    qb1, vb1, dqm1, dvm1 = attention_call(False, 3, *shared, ())
    qb2, vb2, dqm2, dvm2, dvp = attention_call(
        True, 0, *shared, (keys_prior, values_prior, vmt_prior)
    )
    handed = from_behind(dvp, -1)

    tiles = pl.pallas_call(
        gather_kernel,
        out_shape=jax.ShapeDtypeStruct((TILES, 16, HEAD_SIZE), BF16),
        grid_spec=pltpu.PrefetchScalarGridSpec(
            num_scalar_prefetch=1,
            grid=(6,),
            in_specs=[pl.BlockSpec((TOKENS, 2048), lambda i, ids: (0, jnp.minimum(i, 3)))]
            + [whole((RANK, TOKENS))] * 5
            + [whole((3, RANK, LANES)), whole((3, RANK, HEAD_SIZE))] * 2,
            out_specs=pl.BlockSpec((16, 16, HEAD_SIZE), lambda i, ids: (i, 0, 0)),
            scratch_shapes=[pltpu.VMEM((32, 16, HEAD_SIZE), F32)],
        ),
        compiler_params=params(16),
        name="gradients",
    )(ids, normed, dqm1, dqm2, dvm1, dvm2, handed, qb1, vb1, qb2, vb2)

    summed = sum_over_devices(tiles)

    listed_items = RANK * (2 * WIDTH + KV_HEADS * LANES + KV_HEADS * HEAD_SIZE) + WIDTH
    qa, qb, va, vb, gain = pl.pallas_call(
        functools.partial(clip_kernel, math.sqrt(listed_items)),
        out_shape=[
            jax.ShapeDtypeStruct((RANK, WIDTH), F32),
            jax.ShapeDtypeStruct((RANK, KV_HEADS * LANES), F32),
            jax.ShapeDtypeStruct((RANK, WIDTH), F32),
            jax.ShapeDtypeStruct((RANK, KV_HEADS * HEAD_SIZE), F32),
            jax.ShapeDtypeStruct((1, WIDTH), F32),
        ],
        scratch_shapes=[pltpu.VMEM((1, WIDTH), F32)],
        compiler_params=params(16),
        name="clip",
    )(summed, query_down_weight, value_down_weight, scale)
    return (qa, qb, va, vb, gain.reshape(WIDTH))


def solution(mesh):
    placed = P("dp", "seq", None)
    return jax.shard_map(
        shards,
        mesh=mesh,
        in_specs=(placed,) * 5 + (P(),) * 6,
        out_specs=(P(), P(), P(), P(), P()),
        check_vma=False,
    )
```

```python
import functools
import math

import jax
import jax.numpy as jnp
from jax import lax
from jax.experimental import pallas as pl
from jax.experimental.pallas import tpu as pltpu
from jax.sharding import PartitionSpec as P

HEAD_SIZE = 128
TOKENS = 256
HALF = 128
WIDTH = 8192
RANK = 8
KV_HEADS = 6
SHARE = 8
LANES = SHARE * HEAD_SIZE
EPS = 1e-05
FACTOR = 1.0 / math.sqrt(HEAD_SIZE)
LOG2_E = 1.4426950408889634
TILES = 96
QB_TILE = 64
F32 = jnp.float32
BF16 = jnp.bfloat16
BOTH = ("seq", "dp")
MIB = 1024 * 1024


def nn(left, right):
    return jnp.dot(left, right, preferred_element_type=F32)


def nt(left, right):
    return lax.dot_general(left, right, (((1,), (1,)), ((), ())), preferred_element_type=F32)


def norm_kernel(x_ref, down_ref, normed_ref, qm_ref, vm_ref, qmt_ref, vmt_ref):
    step = 1024
    total = jnp.zeros((HALF, HEAD_SIZE), F32)
    for start in range(0, WIDTH, HEAD_SIZE):
        part = x_ref[:, start : start + HEAD_SIZE].astype(F32)
        total = total + part * part
    mean = jnp.sum(total, axis=1, keepdims=True) * (1.0 / WIDTH)
    inverse = lax.rsqrt(mean + EPS)
    mid = jnp.zeros((HALF, 2 * RANK), F32)
    for start in range(0, WIDTH, step):
        cols = slice(start, start + step)
        down = down_ref[:, cols]
        unit = x_ref[:, cols].astype(F32) * inverse
        normed = (unit * down[16:32].astype(F32)[:1]).astype(BF16)
        normed_ref[:, cols] = normed
        mid = mid + nt(normed, down[:16])
    qm_ref[...] = mid[:, :RANK].astype(BF16)
    vm_ref[...] = mid[:, RANK:].astype(BF16)
    mid_t = mid.T
    qmt_ref[...] = mid_t[:RANK].astype(BF16)
    vmt_ref[...] = mid_t[RANK:].astype(BF16)


def pick_kernel(ids_ref, k_ref, v_ref, vm_ref, vmt_ref, vup_ref, keys_ref, values_ref):
    for i in range(3):
        small = head_cols(ids_ref, 3 + i, HEAD_SIZE)
        keys_ref[i] = k_ref[:, small]
        values_ref[i] = adapted(v_ref[:, small], vm_ref[...], vup_ref[:, small])
    mid_t = vmt_ref[...].astype(F32)
    pad = jnp.zeros((RANK, HEAD_SIZE), F32)
    values_ref[3] = jnp.zeros((TOKENS, HEAD_SIZE), BF16)
    for j in range(2):
        block = jnp.concatenate([mid_t[:, j * HEAD_SIZE : (j + 1) * HEAD_SIZE], pad], axis=0)
        values_ref[3, j * 16 : (j + 1) * 16] = block.astype(BF16)


def head_at(ids_ref, place):
    odd = lax.axis_index("seq") % 2
    return jnp.where(odd == 1, ids_ref[(place + 3) % KV_HEADS], ids_ref[place])


def head_cols(ids_ref, place, size):
    return pl.ds(pl.multiple_of(head_at(ids_ref, place) * size, size), size)


def token_rows(c):
    return slice(c * HALF, (c + 1) * HALF)


def stacked(ref, i, c):
    return jnp.concatenate(
        [ref[i, token_rows(c), j * HEAD_SIZE : (j + 1) * HEAD_SIZE] for j in range(SHARE)], axis=0
    )


def stacked_grads(ref, ids_ref, place, c):
    start = head_at(ids_ref, place) * LANES
    return jnp.concatenate(
        [
            ref[token_rows(c), pl.ds(pl.multiple_of(start + j * HEAD_SIZE, HEAD_SIZE), HEAD_SIZE)]
            for j in range(SHARE)
        ],
        axis=0,
    )


def causal_mask():
    key_id = lax.broadcasted_iota(jnp.int32, (HALF, HALF), 0)
    query_id = lax.broadcasted_iota(jnp.int32, (HALF, HALF), 1)
    return jnp.concatenate([key_id <= query_id] * SHARE, axis=1)


def transposed(array):
    return array.astype(F32).T.astype(BF16)


def adapted(frozen, mid, up):
    return (frozen.astype(F32) + 2.0 * nn(mid, up)).astype(BF16)


def own_scores(keys, queries, c, mask):
    own = nt(keys[: (c + 1) * HALF], queries) * (FACTOR * LOG2_E)
    if c == 0:
        return [jnp.where(mask, own, -jnp.inf)]
    return [own[:HALF], jnp.where(mask, own[HALF:], -jnp.inf)]


def softmax(parts):
    top = functools.reduce(jnp.maximum, [jnp.max(s, axis=0, keepdims=True) for s in parts])
    exps = [jnp.exp2(s - top) for s in parts]
    denom = functools.reduce(jnp.add, [jnp.sum(e, axis=0, keepdims=True) for e in exps])
    inv = 1.0 / denom
    return [e * inv for e in exps]


def summed_over_keys(parts):
    return functools.reduce(jnp.add, [jnp.sum(p, axis=0, keepdims=True) for p in parts])


def keep_dq(dq_scr, i, c, dq_t):
    dq_b = (dq_t * FACTOR).astype(BF16)
    for j in range(SHARE):
        dq_scr[i, j * HEAD_SIZE : (j + 1) * HEAD_SIZE, token_rows(c)] = dq_b[:, j * HALF : (j + 1) * HALF]


UNITS = [(i, c) for i in range(3) for c in range(2)]


def pipelined(before, after):
    ahead = before(*UNITS[0])
    for n, unit in enumerate(UNITS):
        state, ahead = ahead, before(*UNITS[n + 1]) if n + 1 < len(UNITS) else None
        after(*unit, state)


def own_kernel(
    ids_ref, q_ref, g_ref, k_ref, v_ref, qm_ref, vm_ref, qmt_ref, vmt_ref, qup_ref, vup_ref,
    qb_ref, vb_ref, dqm_ref, dvm_ref, q_scr, dq_scr,
):
    mask = causal_mask()
    heads = {}
    totals = {}

    def before(i, c):
        if c == 0:
            small = head_cols(ids_ref, 3 + i, HEAD_SIZE)
            keys = k_ref[:, small]
            vup, qup = vup_ref[:, small], qup_ref[:, head_cols(ids_ref, 3 + i, LANES)]
            q_scr[i] = adapted(q_ref[:, head_cols(ids_ref, 3 + i, LANES)], qm_ref[...], qup)
            heads[i] = (keys, transposed(keys), adapted(v_ref[:, small], vm_ref[...], vup), qup, vup)
        keys, _, values, _, _ = heads[i]
        grads = stacked_grads(g_ref, ids_ref, 3 + i, c)
        return own_scores(keys, stacked(q_scr, i, c), c, mask), nt(values[: (c + 1) * HALF], grads), grads

    def after(i, c, state):
        parts, dprob, grads = state
        _, keys_t, _, qup, vup = heads[i]
        probs = softmax(parts)
        dprobs = [dprob[j * HALF : (j + 1) * HALF] for j in range(c + 1)]
        weights = [p.astype(BF16) for p in probs]
        delta = summed_over_keys([w.astype(F32) * d for w, d in zip(weights, dprobs)])
        dscore = [(p * (d - delta)).astype(BF16) for p, d in zip(probs, dprobs)]
        near = (c + 1) * HALF
        keep_dq(dq_scr, i, c, nn(keys_t[:, :near], jnp.concatenate(dscore, axis=0)))
        term = nn(jnp.concatenate(weights, axis=0), grads)
        if c == 0:
            totals["low"] = term
            return
        dv = jnp.concatenate([totals["low"] + term[:HALF], term[HALF:]], axis=0).astype(BF16)
        dq_t = dq_scr[i]
        qb_ref[i] = 2.0 * nt(qmt_ref[...], dq_t)
        vb_ref[i] = 2.0 * nn(vmt_ref[...], dv)
        dq, dv = 2.0 * nn(qup, dq_t), 2.0 * nt(vup, dv)
        totals["dq"] = totals["dq"] + dq if i else dq
        totals["dv"] = totals["dv"] + dv if i else dv

    pipelined(before, after)
    dqm_ref[...] = totals["dq"]
    dvm_ref[...] = totals["dv"]


def weights_kernel(
    ids_ref, q_ref, g_ref, k_ref, qm_ref, vmt_ref, qup_ref, vup_ref, kp_ref, dvm1_ref,
    w_ref, dvp_ref, vb_ref, dvm_ref, handed_ref, q_scr,
):
    mask = causal_mask()
    heads = {}
    totals = {"dv": dvm1_ref[...]}

    def before(i, c):
        if c == 0:
            small = head_cols(ids_ref, i, HEAD_SIZE)
            qup = qup_ref[:, head_cols(ids_ref, i, LANES)]
            q_scr[i] = adapted(q_ref[:, head_cols(ids_ref, i, LANES)], qm_ref[...], qup)
            heads[i] = (k_ref[:, small], kp_ref[i], vup_ref[:, small])
        keys, prior, _ = heads[i]
        queries = stacked(q_scr, i, c)
        return own_scores(keys, queries, c, mask), nt(prior, queries) * (FACTOR * LOG2_E)

    def after(i, c, state):
        own, prior = state
        probs = softmax(own + [prior])
        weights = jnp.concatenate([p.astype(BF16) for p in probs], axis=0)
        rows = 3 * HALF + c * HALF
        w_ref[i, c * 3 * HALF : c * 3 * HALF + rows] = weights
        grads = stacked_grads(g_ref, ids_ref, i, c)
        term = nn(weights, grads)
        if c == 0:
            totals["low"] = term
            return
        low = totals["low"]
        dv = jnp.concatenate([low[:HALF] + term[:HALF], term[HALF : 2 * HALF]], axis=0).astype(BF16)
        dv_prior = (low[HALF:] + term[2 * HALF :]).astype(BF16)
        _, _, vup = heads[i]
        dvp_ref[i] = dv_prior
        vb_ref[i] = 2.0 * nn(vmt_ref[...], dv)
        totals["dv"] = totals["dv"] + 2.0 * nt(vup, dv)
        handed = 2.0 * nt(vup, dv_prior)
        totals["handed"] = totals["handed"] + handed if i else handed

    pipelined(before, after)
    dvm_ref[...] = totals["dv"]
    handed_ref[...] = totals["handed"]


def dscore_kernel(
    ids_ref, g_ref, k_ref, v_ref, vm_ref, qmt_ref, qup_ref, vup_ref, kp_ref, vp_ref,
    w_ref, dvp_ref, vb1_ref, dqm1_ref, qb_ref, vb_ref, dqm_ref, dq_scr,
):
    vmt_prior = jnp.concatenate(
        [vp_ref[3, j * 16 : (j + 1) * 16].astype(F32)[:RANK] for j in range(2)], axis=1
    ).astype(BF16)
    heads = {}
    totals = {"dq": dqm1_ref[...]}

    def before(i, c):
        if c == 0:
            small = head_cols(ids_ref, i, HEAD_SIZE)
            vup = vup_ref[:, small]
            heads[i] = (
                transposed(k_ref[:, small]),
                transposed(kp_ref[i]),
                adapted(v_ref[:, small], vm_ref[...], vup),
                vp_ref[i],
            )
        _, _, values, prior = heads[i]
        grads = stacked_grads(g_ref, ids_ref, i, c)
        return nt(values[: (c + 1) * HALF], grads), nt(prior, grads)

    def after(i, c, dprobs):
        keys_t, prior_t, _, _ = heads[i]
        near = (c + 1) * HALF
        start = c * 3 * HALF
        weights = [
            w_ref[i, start : start + near].astype(F32),
            w_ref[i, start + near : start + near + TOKENS].astype(F32),
        ]
        delta = summed_over_keys([w * d for w, d in zip(weights, dprobs)])
        dscore = [(w * (d - delta)).astype(BF16) for w, d in zip(weights, dprobs)]
        keep_dq(dq_scr, i, c, nn(keys_t[:, :near], dscore[0]) + nn(prior_t, dscore[1]))
        if c == 0:
            return
        dq_t = dq_scr[i]
        qb_ref[i] = 2.0 * nt(qmt_ref[...], dq_t)
        vb_ref[i] = vb1_ref[i] + 2.0 * nn(vmt_prior, dvp_ref[i])
        totals["dq"] = totals["dq"] + 2.0 * nn(qup_ref[:, head_cols(ids_ref, i, LANES)], dq_t)

    pipelined(before, after)
    dqm_ref[...] = totals["dq"]


def gather_kernel(
    ids_ref, normed_ref, dqm_ref, dvm_ref, dvh_ref,
    qb1_ref, vb1_ref, qb2_ref, vb2_ref, out_ref, buf,
):
    step = pl.program_id(0)

    @pl.when(step < 4)
    def _():
        dq = dqm_ref[...]
        dv = dvm_ref[...] + dvh_ref[...]
        mids = jnp.concatenate([dq, dv], axis=0).astype(BF16)
        for j in range(4):
            part = nn(mids, normed_ref[:, j * 512 : (j + 1) * 512]).astype(BF16)
            for k in range(4):
                out_ref[4 * j + k] = part[:, k * HEAD_SIZE : (k + 1) * HEAD_SIZE]

    @pl.when(step == 4)
    def _():
        buf[27:32] = jnp.zeros((5, 16, HEAD_SIZE), F32)
        for i in range(3):
            for base, qb_ref, vb_ref in ((0, qb2_ref, vb2_ref), (3, qb1_ref, vb1_ref)):
                head = head_at(ids_ref, base + i)
                upper = head >= 3
                row = pl.multiple_of(jnp.where(upper, 8, 0), 8)
                place = jnp.where(upper, head - 3, head)
                for k in range(SHARE):
                    buf[place * SHARE + k, pl.ds(row, 8), :] = qb_ref[i][:, k * HEAD_SIZE : (k + 1) * HEAD_SIZE]
                buf[24 + place, pl.ds(row, 8), :] = vb_ref[i]
        for t in range(16):
            out_ref[t] = buf[t].astype(BF16)

    @pl.when(step == 5)
    def _():
        for t in range(16):
            out_ref[t] = buf[16 + t].astype(BF16)


def clip_kernel(limit, sum_ref, qd_ref, vd_ref, scale_ref, qa_ref, qb_ref, va_ref, vb_ref, gain_ref, gains):
    total = jnp.zeros((16, HEAD_SIZE), F32)
    gain_total = jnp.zeros((1, HEAD_SIZE), F32)
    for t in range(QB_TILE):
        cols = slice(t * HEAD_SIZE, (t + 1) * HEAD_SIZE)
        tile = sum_ref[t].astype(F32)
        total = total + tile * tile
        mixed = qd_ref[:, cols].astype(F32) * tile[:RANK] + vd_ref[:, cols].astype(F32) * tile[RANK:]
        gain = jnp.sum(mixed, axis=0, keepdims=True) / scale_ref[:, cols].astype(F32)
        gains[:, cols] = gain
        gain_total = gain_total + gain * gain
    for t in range(QB_TILE, QB_TILE + 27):
        tile = sum_ref[t].astype(F32)
        total = total + tile * tile
    squares = jnp.sum(total, keepdims=True) + jnp.sum(gain_total, keepdims=True)
    factor = jnp.minimum(1.0, limit / jnp.sqrt(squares))
    gain_ref[...] = gains[...] * factor
    for t in range(QB_TILE):
        cols = slice(t * HEAD_SIZE, (t + 1) * HEAD_SIZE)
        tile = sum_ref[t].astype(F32) * factor
        qa_ref[:, cols] = tile[:RANK]
        va_ref[:, cols] = tile[RANK:]
    for t in range(24):
        tile = sum_ref[QB_TILE + t].astype(F32) * factor
        qb_ref[:, t * HEAD_SIZE : (t + 1) * HEAD_SIZE] = tile[:RANK]
        qb_ref[:, (24 + t) * HEAD_SIZE : (25 + t) * HEAD_SIZE] = tile[RANK:]
    for t in range(3):
        tile = sum_ref[QB_TILE + 24 + t].astype(F32) * factor
        vb_ref[:, t * HEAD_SIZE : (t + 1) * HEAD_SIZE] = tile[:RANK]
        vb_ref[:, (3 + t) * HEAD_SIZE : (4 + t) * HEAD_SIZE] = tile[RANK:]


def groups_along(keys):
    found = {}
    for device in range(256):
        y, xh, z, rest = device // 64, device // 32 % 2, device // 4 % 8, device % 4
        place = {"y": y, "xh": xh, "z": z, "xl": rest // 2, "core": rest % 2}
        found.setdefault(tuple(v for k, v in place.items() if k not in keys), []).append(device)
    return list(found.values())


PLANE = groups_along(("y", "xh", "xl", "core"))
COLUMN = groups_along(("z",))


def exchange(array, groups):
    return lax.all_to_all(array, BOTH, 0, 0, tiled=True, axis_index_groups=groups)


def sum_over_devices(tiles):
    shares = tiles.reshape(32, 3, 16, HEAD_SIZE)
    mine = jnp.sum(exchange(shares, PLANE).astype(F32), axis=0).astype(BF16)
    copies = jnp.broadcast_to(mine[None], (8, 3, 16, HEAD_SIZE))
    mine = jnp.sum(exchange(copies, COLUMN).astype(F32), axis=0).astype(BF16)
    copies = jnp.broadcast_to(mine[None], (32, 3, 16, HEAD_SIZE))
    return exchange(copies, PLANE).reshape(TILES, 16, HEAD_SIZE)


def from_behind(block, distance):
    return lax.ppermute(block, "seq", [((i - distance) % 8, i) for i in range(8)])


def whole(shape):
    return pl.BlockSpec(shape, lambda *_: (0,) * len(shape))


def params(mib):
    return pltpu.CompilerParams(vmem_limit_bytes=mib * MIB)


def struct(shape, dtype):
    return jax.ShapeDtypeStruct(shape, dtype)


VMEM = pl.BlockSpec(memory_space=pltpu.VMEM)
SMEM = pl.BlockSpec(memory_space=pltpu.SMEM)
HBM = pl.BlockSpec(memory_space=pl.ANY)


def cost(us):
    return pl.CostEstimate(flops=int(us * 1e9), bytes_accessed=0, transcendentals=0)


def own_call(ids, q, g, k, v, qm, vm, qmt, vmt, qup, vup):
    return pl.pallas_call(
        own_kernel,
        out_shape=[
            struct((3, RANK, LANES), F32), struct((3, RANK, HEAD_SIZE), F32),
            struct((RANK, TOKENS), F32), struct((RANK, TOKENS), F32),
        ],
        in_specs=[SMEM] + [VMEM] * 10,
        out_specs=[VMEM] * 4,
        scratch_shapes=[pltpu.VMEM((3, TOKENS, LANES), BF16), pltpu.VMEM((3, LANES, TOKENS), BF16)],
        compiler_params=params(28),
        cost_estimate=cost(1),
        name="own_attention",
    )(ids, q, g, k, v, qm, vm, qmt, vmt, qup, vup)


def weights_call(ids, q, g, k, qm, vmt, qup, vup, kv_prior, dvm):
    return pl.pallas_call(
        weights_kernel,
        out_shape=[
            struct((3, 7 * HALF, LANES), BF16), struct((3, TOKENS, HEAD_SIZE), BF16),
            struct((3, RANK, HEAD_SIZE), F32), struct((RANK, TOKENS), F32), struct((RANK, TOKENS), F32),
        ],
        in_specs=[SMEM] + [VMEM] * 9,
        out_specs=[VMEM] * 5,
        scratch_shapes=[pltpu.VMEM((3, TOKENS, LANES), BF16)],
        compiler_params=params(32),
        cost_estimate=cost(4),
        name="prior_weights",
    )(ids, q, g, k, qm, vmt, qup, vup, kv_prior, dvm)


def dscore_call(ids, g, k, v, vm, qmt, qup, vup, kv_prior, vmt_prior, w, dvp, vb, dqm):
    return pl.pallas_call(
        dscore_kernel,
        out_shape=[
            struct((3, RANK, LANES), F32), struct((3, RANK, HEAD_SIZE), F32), struct((RANK, TOKENS), F32),
        ],
        in_specs=[SMEM] + [VMEM] * 13,
        out_specs=[VMEM] * 3,
        scratch_shapes=[pltpu.VMEM((3, LANES, TOKENS), BF16)],
        compiler_params=params(32),
        cost_estimate=cost(4),
        name="prior_dscore",
    )(ids, g, k, v, vm, qmt, qup, vup, kv_prior, vmt_prior, w, dvp, vb, dqm)


def shards(
    layer_input,
    frozen_queries,
    frozen_keys,
    frozen_values,
    output_gradient,
    norm_scale_vector,
    query_down_weight,
    query_up_weight,
    value_down_weight,
    value_up_weight,
    head_ordering,
):
    x, q, k, v, g = (
        a[0] for a in (layer_input, frozen_queries, frozen_keys, frozen_values, output_gradient)
    )
    ids, qup, vup = head_ordering, query_up_weight, value_up_weight
    scale = norm_scale_vector.reshape(1, WIDTH)
    down = jnp.concatenate(
        [query_down_weight, value_down_weight, jnp.broadcast_to(scale, (16, WIDTH))], axis=0
    )

    normed, qm, vm, qmt, vmt = pl.pallas_call(
        norm_kernel,
        out_shape=[
            struct((TOKENS, WIDTH), BF16), struct((TOKENS, RANK), BF16), struct((TOKENS, RANK), BF16),
            struct((RANK, TOKENS), BF16), struct((RANK, TOKENS), BF16),
        ],
        grid=(2,),
        in_specs=[pl.BlockSpec((HALF, WIDTH), lambda i: (i, 0)), whole((32, WIDTH))],
        out_specs=[
            pl.BlockSpec((HALF, WIDTH), lambda i: (i, 0)),
            pl.BlockSpec((HALF, RANK), lambda i: (i, 0)),
            pl.BlockSpec((HALF, RANK), lambda i: (i, 0)),
            pl.BlockSpec((RANK, HALF), lambda i: (0, i)),
            pl.BlockSpec((RANK, HALF), lambda i: (0, i)),
        ],
        compiler_params=params(20),
        cost_estimate=cost(5),
        name="norm",
    )(x, down)

    keys_out, values_out = pl.pallas_call(
        pick_kernel,
        out_shape=[struct((3, TOKENS, HEAD_SIZE), BF16), struct((4, TOKENS, HEAD_SIZE), BF16)],
        in_specs=[SMEM] + [VMEM] * 5,
        out_specs=[VMEM] * 2,
        compiler_params=params(8),
        name="pick",
    )(ids, k, v, vm, vmt, vup)
    keys_prior = from_behind(keys_out, 1)
    values_prior = from_behind(values_out, 1)

    qb1, vb1, dqm1, dvm1 = own_call(ids, q, g, k, v, qm, vm, qmt, vmt, qup, vup)
    w, dvp, vbp, dvm, handed = weights_call(ids, q, g, k, qm, vmt, qup, vup, keys_prior, dvm1)
    handed = from_behind(handed, -1)
    qb2, vb2, dqm = dscore_call(
        ids, g, k, v, vm, qmt, qup, vup, keys_prior, values_prior, w, dvp, vbp, dqm1
    )

    tiles = pl.pallas_call(
        gather_kernel,
        out_shape=jax.ShapeDtypeStruct((TILES, 16, HEAD_SIZE), BF16),
        grid_spec=pltpu.PrefetchScalarGridSpec(
            num_scalar_prefetch=1,
            grid=(6,),
            in_specs=[pl.BlockSpec((TOKENS, 2048), lambda i, ids: (0, jnp.minimum(i, 3)))]
            + [whole((RANK, TOKENS))] * 3
            + [whole((3, RANK, LANES)), whole((3, RANK, HEAD_SIZE))] * 2,
            out_specs=pl.BlockSpec((16, 16, HEAD_SIZE), lambda i, ids: (i, 0, 0)),
            scratch_shapes=[pltpu.VMEM((32, 16, HEAD_SIZE), F32)],
        ),
        compiler_params=params(16),
        name="gradients",
    )(ids, normed, dqm, dvm, handed, qb1, vb1, qb2, vb2)

    summed = sum_over_devices(tiles)

    listed_items = RANK * (2 * WIDTH + KV_HEADS * LANES + KV_HEADS * HEAD_SIZE) + WIDTH
    qa, qb, va, vb, gain = pl.pallas_call(
        functools.partial(clip_kernel, math.sqrt(listed_items)),
        out_shape=[
            jax.ShapeDtypeStruct((RANK, WIDTH), F32),
            jax.ShapeDtypeStruct((RANK, KV_HEADS * LANES), F32),
            jax.ShapeDtypeStruct((RANK, WIDTH), F32),
            jax.ShapeDtypeStruct((RANK, KV_HEADS * HEAD_SIZE), F32),
            jax.ShapeDtypeStruct((1, WIDTH), F32),
        ],
        scratch_shapes=[pltpu.VMEM((1, WIDTH), F32)],
        compiler_params=params(16),
        name="clip",
    )(summed, query_down_weight, value_down_weight, scale)
    return (qa, qb, va, vb, gain.reshape(WIDTH))


def solution(mesh):
    placed = P("dp", "seq", None)
    return jax.shard_map(
        shards,
        mesh=mesh,
        in_specs=(placed,) * 5 + (P(),) * 6,
        out_specs=(P(), P(), P(), P(), P()),
        check_vma=False,
    )
```

```python
import functools
import math

import jax
import jax.numpy as jnp
from jax import lax
from jax.experimental import pallas as pl
from jax.experimental.pallas import tpu as pltpu
from jax.sharding import PartitionSpec as P

HEAD_SIZE = 128
TOKENS = 256
HALF = 128
WIDTH = 8192
RANK = 8
KV_HEADS = 6
SHARE = 8
LANES = SHARE * HEAD_SIZE
EPS = 1e-05
FACTOR = 1.0 / math.sqrt(HEAD_SIZE)
LOG2_E = 1.4426950408889634
TILES = 96
QB_TILE = 64
PART = TILES // 2
F32 = jnp.float32
BF16 = jnp.bfloat16
BOTH = ("seq", "dp")
MIB = 1024 * 1024


def nn(left, right):
    return jnp.dot(left, right, preferred_element_type=F32)


def nt(left, right):
    return lax.dot_general(left, right, (((1,), (1,)), ((), ())), preferred_element_type=F32)


def norm_kernel(x_ref, down_ref, normed_ref, qm_ref, vm_ref, qmt_ref, vmt_ref):
    step = 1024
    total = jnp.zeros((HALF, HEAD_SIZE), F32)
    for start in range(0, WIDTH, HEAD_SIZE):
        part = x_ref[:, start : start + HEAD_SIZE].astype(F32)
        total = total + part * part
    mean = jnp.sum(total, axis=1, keepdims=True) * (1.0 / WIDTH)
    inverse = lax.rsqrt(mean + EPS)
    mid = jnp.zeros((HALF, 2 * RANK), F32)
    for start in range(0, WIDTH, step):
        cols = slice(start, start + step)
        down = down_ref[:, cols]
        unit = x_ref[:, cols].astype(F32) * inverse
        normed = (unit * down[16:32].astype(F32)[:1]).astype(BF16)
        normed_ref[:, cols] = normed
        mid = mid + nt(normed, down[:16])
    qm_ref[...] = mid[:, :RANK].astype(BF16)
    vm_ref[...] = mid[:, RANK:].astype(BF16)
    mid_t = mid.T
    qmt_ref[...] = mid_t[:RANK].astype(BF16)
    vmt_ref[...] = mid_t[RANK:].astype(BF16)


def pick_kernel(ids_ref, k_ref, v_ref, vm_ref, vmt_ref, vup_ref, keys_ref, values_ref):
    for i in range(3):
        small = head_cols(ids_ref, 3 + i, HEAD_SIZE)
        keys_ref[i] = k_ref[:, small]
        values_ref[i] = adapted(v_ref[:, small], vm_ref[...], vup_ref[:, small])
    mid_t = vmt_ref[...].astype(F32)
    pad = jnp.zeros((RANK, HEAD_SIZE), F32)
    values_ref[3] = jnp.zeros((TOKENS, HEAD_SIZE), BF16)
    for j in range(2):
        block = jnp.concatenate([mid_t[:, j * HEAD_SIZE : (j + 1) * HEAD_SIZE], pad], axis=0)
        values_ref[3, j * 16 : (j + 1) * 16] = block.astype(BF16)


def head_at(ids_ref, place):
    odd = lax.axis_index("seq") % 2
    return jnp.where(odd == 1, ids_ref[(place + 3) % KV_HEADS], ids_ref[place])


def head_cols(ids_ref, place, size):
    return pl.ds(pl.multiple_of(head_at(ids_ref, place) * size, size), size)


def token_rows(c):
    return slice(c * HALF, (c + 1) * HALF)


def share(part):
    return range(part * WIDE, (part + 1) * WIDE)


def stacked(ref, i, c, part):
    return jnp.concatenate(
        [ref[i, token_rows(c), j * HEAD_SIZE : (j + 1) * HEAD_SIZE] for j in share(part)], axis=0
    )


def stacked_grads(ref, ids_ref, place, c, part):
    start = head_at(ids_ref, place) * LANES
    return jnp.concatenate(
        [
            ref[token_rows(c), pl.ds(pl.multiple_of(start + j * HEAD_SIZE, HEAD_SIZE), HEAD_SIZE)]
            for j in share(part)
        ],
        axis=0,
    )


def causal_mask():
    key_id = lax.broadcasted_iota(jnp.int32, (HALF, HALF), 0)
    query_id = lax.broadcasted_iota(jnp.int32, (HALF, HALF), 1)
    return jnp.concatenate([key_id <= query_id] * WIDE, axis=1)


def transposed(array):
    return array.astype(F32).T.astype(BF16)


def adapted(frozen, mid, up):
    return (frozen.astype(F32) + 2.0 * nn(mid, up)).astype(BF16)


def own_scores(keys, queries, c, mask):
    own = nt(keys[: (c + 1) * HALF], queries) * (FACTOR * LOG2_E)
    if c == 0:
        return [jnp.where(mask, own, -jnp.inf)]
    return [own[:HALF], jnp.where(mask, own[HALF:], -jnp.inf)]


def softmax(parts):
    top = functools.reduce(jnp.maximum, [jnp.max(s, axis=0, keepdims=True) for s in parts])
    exps = [jnp.exp2(s - top) for s in parts]
    denom = functools.reduce(jnp.add, [jnp.sum(e, axis=0, keepdims=True) for e in exps])
    inv = 1.0 / denom
    return [e * inv for e in exps]


def summed_over_keys(parts):
    return functools.reduce(jnp.add, [jnp.sum(p, axis=0, keepdims=True) for p in parts])


def keep_dq(dq_scr, i, c, part, dq_t):
    dq_b = (dq_t * FACTOR).astype(BF16)
    for n, j in enumerate(share(part)):
        dq_scr[i, j * HEAD_SIZE : (j + 1) * HEAD_SIZE, token_rows(c)] = dq_b[:, n * HALF : (n + 1) * HALF]


def accumulate(totals, name, first, value):
    totals[name] = value if first else totals[name] + value


WIDE = 2
AHEAD = 4
UNITS = [(i, c, part) for i in range(3) for c in range(2) for part in range(SHARE // WIDE)]


def pipelined(before, after):
    states = [before(*unit) for unit in UNITS[:AHEAD]]
    for n, unit in enumerate(UNITS):
        if n + AHEAD < len(UNITS):
            states.append(before(*UNITS[n + AHEAD]))
        after(*unit, states.pop(0))


def own_kernel(
    ids_ref, q_ref, g_ref, k_ref, v_ref, qm_ref, vm_ref, qmt_ref, vmt_ref, qup_ref, vup_ref,
    qb_ref, vb_ref, dqm_ref, dvm_ref, q_scr, dq_scr,
):
    mask = causal_mask()
    heads = {}
    totals = {}

    def before(i, c, part):
        if c == 0 and part == 0:
            small = head_cols(ids_ref, 3 + i, HEAD_SIZE)
            keys = k_ref[:, small]
            vup, qup = vup_ref[:, small], qup_ref[:, head_cols(ids_ref, 3 + i, LANES)]
            q_scr[i] = adapted(q_ref[:, head_cols(ids_ref, 3 + i, LANES)], qm_ref[...], qup)
            heads[i] = (keys, transposed(keys), adapted(v_ref[:, small], vm_ref[...], vup), qup, vup)
        keys, _, values, _, _ = heads[i]
        grads = stacked_grads(g_ref, ids_ref, 3 + i, c, part)
        return own_scores(keys, stacked(q_scr, i, c, part), c, mask), nt(values[: (c + 1) * HALF], grads), grads

    def after(i, c, part, state):
        parts, dprob, grads = state
        _, keys_t, _, qup, vup = heads[i]
        probs = softmax(parts)
        dprobs = [dprob[j * HALF : (j + 1) * HALF] for j in range(c + 1)]
        weights = [p.astype(BF16) for p in probs]
        delta = summed_over_keys([w.astype(F32) * d for w, d in zip(weights, dprobs)])
        dscore = [(p * (d - delta)).astype(BF16) for p, d in zip(probs, dprobs)]
        near = (c + 1) * HALF
        keep_dq(dq_scr, i, c, part, nn(keys_t[:, :near], jnp.concatenate(dscore, axis=0)))
        term = nn(jnp.concatenate(weights, axis=0), grads)
        accumulate(totals, "low", c == 0 and part == 0, term[:HALF])
        if c == 0:
            return
        accumulate(totals, "high", part == 0, term[HALF:])
        if part < SHARE // WIDE - 1:
            return
        dv = jnp.concatenate([totals["low"], totals["high"]], axis=0).astype(BF16)
        dq_t = dq_scr[i]
        qb_ref[i] = 2.0 * nt(qmt_ref[...], dq_t)
        vb_ref[i] = 2.0 * nn(vmt_ref[...], dv)
        dq, dv = 2.0 * nn(qup, dq_t), 2.0 * nt(vup, dv)
        totals["dq"] = totals["dq"] + dq if i else dq
        totals["dv"] = totals["dv"] + dv if i else dv

    pipelined(before, after)
    dqm_ref[...] = totals["dq"]
    dvm_ref[...] = totals["dv"]


def weights_kernel(
    ids_ref, q_ref, g_ref, k_ref, qm_ref, vmt_ref, qup_ref, vup_ref, kp_ref, dvm1_ref,
    w_ref, dvp_ref, vb_ref, dvm_ref, handed_ref, q_scr,
):
    mask = causal_mask()
    heads = {}
    totals = {"dv": dvm1_ref[...]}

    def before(i, c, part):
        if c == 0 and part == 0:
            small = head_cols(ids_ref, i, HEAD_SIZE)
            qup = qup_ref[:, head_cols(ids_ref, i, LANES)]
            q_scr[i] = adapted(q_ref[:, head_cols(ids_ref, i, LANES)], qm_ref[...], qup)
            heads[i] = (k_ref[:, small], kp_ref[i], vup_ref[:, small])
        keys, prior, _ = heads[i]
        queries = stacked(q_scr, i, c, part)
        return own_scores(keys, queries, c, mask), nt(prior, queries) * (FACTOR * LOG2_E)

    def after(i, c, part, state):
        own, prior = state
        probs = softmax(own + [prior])
        weights = jnp.concatenate([p.astype(BF16) for p in probs], axis=0)
        rows = 3 * HALF + c * HALF
        w_ref[i, c * 3 * HALF : c * 3 * HALF + rows, part * WIDE * HALF : (part + 1) * WIDE * HALF] = weights
        grads = stacked_grads(g_ref, ids_ref, i, c, part)
        term = nn(weights, grads)
        near = (c + 1) * HALF
        accumulate(totals, "low", c == 0 and part == 0, term[:HALF])
        accumulate(totals, "prior", c == 0 and part == 0, term[near:])
        if c == 0:
            return
        accumulate(totals, "high", part == 0, term[HALF:near])
        if part < SHARE // WIDE - 1:
            return
        dv = jnp.concatenate([totals["low"], totals["high"]], axis=0).astype(BF16)
        dv_prior = totals["prior"].astype(BF16)
        _, _, vup = heads[i]
        dvp_ref[i] = dv_prior
        vb_ref[i] = 2.0 * nn(vmt_ref[...], dv)
        totals["dv"] = totals["dv"] + 2.0 * nt(vup, dv)
        handed = 2.0 * nt(vup, dv_prior)
        totals["handed"] = totals["handed"] + handed if i else handed

    pipelined(before, after)
    dvm_ref[...] = totals["dv"]
    handed_ref[...] = totals["handed"]


def dscore_kernel(
    ids_ref, g_ref, k_ref, v_ref, vm_ref, qmt_ref, qup_ref, vup_ref, kp_ref, vp_ref,
    w_ref, dvp_ref, vb1_ref, dqm1_ref, qb_ref, vb_ref, dqm_ref, dq_scr,
):
    vmt_prior = jnp.concatenate(
        [vp_ref[3, j * 16 : (j + 1) * 16].astype(F32)[:RANK] for j in range(2)], axis=1
    ).astype(BF16)
    heads = {}
    totals = {"dq": dqm1_ref[...]}

    def before(i, c, part):
        if c == 0 and part == 0:
            small = head_cols(ids_ref, i, HEAD_SIZE)
            vup = vup_ref[:, small]
            heads[i] = (
                transposed(k_ref[:, small]),
                transposed(kp_ref[i]),
                adapted(v_ref[:, small], vm_ref[...], vup),
                vp_ref[i],
            )
        _, _, values, prior = heads[i]
        grads = stacked_grads(g_ref, ids_ref, i, c, part)
        return nt(values[: (c + 1) * HALF], grads), nt(prior, grads)

    def after(i, c, part, dprobs):
        keys_t, prior_t, _, _ = heads[i]
        near = (c + 1) * HALF
        start = c * 3 * HALF
        cols = slice(part * WIDE * HALF, (part + 1) * WIDE * HALF)
        weights = [
            w_ref[i, start : start + near, cols].astype(F32),
            w_ref[i, start + near : start + near + TOKENS, cols].astype(F32),
        ]
        delta = summed_over_keys([w * d for w, d in zip(weights, dprobs)])
        dscore = [(w * (d - delta)).astype(BF16) for w, d in zip(weights, dprobs)]
        keep_dq(dq_scr, i, c, part, nn(keys_t[:, :near], dscore[0]) + nn(prior_t, dscore[1]))
        if c == 0 or part < SHARE // WIDE - 1:
            return
        dq_t = dq_scr[i]
        qb_ref[i] = 2.0 * nt(qmt_ref[...], dq_t)
        vb_ref[i] = vb1_ref[i] + 2.0 * nn(vmt_prior, dvp_ref[i])
        totals["dq"] = totals["dq"] + 2.0 * nn(qup_ref[:, head_cols(ids_ref, i, LANES)], dq_t)

    pipelined(before, after)
    dqm_ref[...] = totals["dq"]


def gather_kernel(
    ids_ref, normed_ref, dqm_ref, dvm_ref, dvh_ref, qb1_ref, vb1_ref, qb2_ref, vb2_ref,
    keep_ref, send_ref, tiles, buf,
):
    mids = jnp.concatenate([dqm_ref[...], dvm_ref[...] + dvh_ref[...]], axis=0).astype(BF16)
    buf[27:32] = jnp.zeros((5, 16, HEAD_SIZE), F32)
    for i in range(3):
        for base, qb_ref, vb_ref in ((0, qb2_ref, vb2_ref), (3, qb1_ref, vb1_ref)):
            head = head_at(ids_ref, base + i)
            upper = head >= 3
            row = pl.multiple_of(jnp.where(upper, 8, 0), 8)
            place = jnp.where(upper, head - 3, head)
            for k in range(SHARE):
                buf[place * SHARE + k, pl.ds(row, 8), :] = qb_ref[i][:, k * HEAD_SIZE : (k + 1) * HEAD_SIZE]
            buf[24 + place, pl.ds(row, 8), :] = vb_ref[i]
    for j in range(16):
        part = nn(mids, normed_ref[:, j * 512 : (j + 1) * 512]).astype(BF16)
        for k in range(4):
            t = 4 * j + k
            tiles[t // PART, t % PART] = part[:, k * HEAD_SIZE : (k + 1) * HEAD_SIZE]
    for t in range(QB_TILE, TILES):
        tiles[t // PART, t % PART] = buf[t - QB_TILE].astype(BF16)
    core = lax.axis_index("dp") % 2
    keep_ref[...] = tiles[core]
    send_ref[...] = tiles[1 - core]


def clip_kernel(
    limit, mine_ref, other_ref, qd_ref, vd_ref, scale_ref,
    qa_ref, qb_ref, va_ref, vb_ref, gain_ref, gains, both,
):
    core = lax.axis_index("dp") % 2
    both[core] = mine_ref[...]
    both[1 - core] = other_ref[...]

    def summed(t):
        return both[t // PART, t % PART].astype(F32)

    total = jnp.zeros((16, HEAD_SIZE), F32)
    gain_total = jnp.zeros((1, HEAD_SIZE), F32)
    for t in range(QB_TILE):
        cols = slice(t * HEAD_SIZE, (t + 1) * HEAD_SIZE)
        tile = summed(t)
        total = total + tile * tile
        mixed = qd_ref[:, cols].astype(F32) * tile[:RANK] + vd_ref[:, cols].astype(F32) * tile[RANK:]
        gain = jnp.sum(mixed, axis=0, keepdims=True) / scale_ref[:, cols].astype(F32)
        gains[:, cols] = gain
        gain_total = gain_total + gain * gain
    for t in range(QB_TILE, QB_TILE + 27):
        tile = summed(t)
        total = total + tile * tile
    squares = jnp.sum(total, keepdims=True) + jnp.sum(gain_total, keepdims=True)
    factor = jnp.minimum(1.0, limit / jnp.sqrt(squares))
    gain_ref[...] = gains[...] * factor
    for t in range(QB_TILE):
        cols = slice(t * HEAD_SIZE, (t + 1) * HEAD_SIZE)
        tile = summed(t) * factor
        qa_ref[:, cols] = tile[:RANK]
        va_ref[:, cols] = tile[RANK:]
    for t in range(24):
        tile = summed(QB_TILE + t) * factor
        qb_ref[:, t * HEAD_SIZE : (t + 1) * HEAD_SIZE] = tile[:RANK]
        qb_ref[:, (24 + t) * HEAD_SIZE : (25 + t) * HEAD_SIZE] = tile[RANK:]
    for t in range(3):
        tile = summed(QB_TILE + 24 + t) * factor
        vb_ref[:, t * HEAD_SIZE : (t + 1) * HEAD_SIZE] = tile[:RANK]
        vb_ref[:, (3 + t) * HEAD_SIZE : (4 + t) * HEAD_SIZE] = tile[RANK:]


def groups_along(keys):
    found = {}
    for device in range(256):
        y, xh, z, rest = device // 64, device // 32 % 2, device // 4 % 8, device % 4
        place = {"y": y, "xh": xh, "z": z, "xl": rest // 2, "core": rest % 2}
        found.setdefault(tuple(v for k, v in place.items() if k not in keys), []).append(device)
    return list(found.values())


PLANE = groups_along(("y", "xh", "xl"))
COLUMN = groups_along(("z",))


def exchange(array, groups):
    return lax.all_to_all(array, BOTH, 0, 0, tiled=True, axis_index_groups=groups)


def other_core(array):
    return lax.ppermute(array, "dp", [(i, i ^ 1) for i in range(32)])


def sum_over_devices(keep, send):
    shares = (keep.astype(F32) + other_core(send).astype(F32)).astype(BF16)
    shares = shares.reshape(16, 3, 16, HEAD_SIZE)
    mine = jnp.sum(exchange(shares, PLANE).astype(F32), axis=0).astype(BF16)
    copies = jnp.broadcast_to(mine[None], (8, 3, 16, HEAD_SIZE))
    mine = jnp.sum(exchange(copies, COLUMN).astype(F32), axis=0).astype(BF16)
    copies = jnp.broadcast_to(mine[None], (16, 3, 16, HEAD_SIZE))
    whole_part = exchange(copies, PLANE).reshape(PART, 16, HEAD_SIZE)
    return whole_part, other_core(whole_part)


def from_behind(block, distance):
    return lax.ppermute(block, "seq", [((i - distance) % 8, i) for i in range(8)])


def whole(shape):
    return pl.BlockSpec(shape, lambda *_: (0,) * len(shape))


def params(mib):
    return pltpu.CompilerParams(vmem_limit_bytes=mib * MIB)


def struct(shape, dtype):
    return jax.ShapeDtypeStruct(shape, dtype)


VMEM = pl.BlockSpec(memory_space=pltpu.VMEM)
SMEM = pl.BlockSpec(memory_space=pltpu.SMEM)
HBM = pl.BlockSpec(memory_space=pl.ANY)


def cost(us):
    return pl.CostEstimate(flops=int(us * 1e9), bytes_accessed=0, transcendentals=0)


def own_call(ids, q, g, k, v, qm, vm, qmt, vmt, qup, vup):
    return pl.pallas_call(
        own_kernel,
        out_shape=[
            struct((3, RANK, LANES), F32), struct((3, RANK, HEAD_SIZE), F32),
            struct((RANK, TOKENS), F32), struct((RANK, TOKENS), F32),
        ],
        in_specs=[SMEM] + [VMEM] * 10,
        out_specs=[VMEM] * 4,
        scratch_shapes=[pltpu.VMEM((3, TOKENS, LANES), BF16), pltpu.VMEM((3, LANES, TOKENS), BF16)],
        compiler_params=params(28),
        cost_estimate=cost(1),
        name="own_attention",
    )(ids, q, g, k, v, qm, vm, qmt, vmt, qup, vup)


def weights_call(ids, q, g, k, qm, vmt, qup, vup, kv_prior, dvm):
    return pl.pallas_call(
        weights_kernel,
        out_shape=[
            struct((3, 7 * HALF, LANES), BF16), struct((3, TOKENS, HEAD_SIZE), BF16),
            struct((3, RANK, HEAD_SIZE), F32), struct((RANK, TOKENS), F32), struct((RANK, TOKENS), F32),
        ],
        in_specs=[SMEM] + [VMEM] * 9,
        out_specs=[VMEM] * 5,
        scratch_shapes=[pltpu.VMEM((3, TOKENS, LANES), BF16)],
        compiler_params=params(32),
        cost_estimate=cost(4),
        name="prior_weights",
    )(ids, q, g, k, qm, vmt, qup, vup, kv_prior, dvm)


def dscore_call(ids, g, k, v, vm, qmt, qup, vup, kv_prior, vmt_prior, w, dvp, vb, dqm):
    return pl.pallas_call(
        dscore_kernel,
        out_shape=[
            struct((3, RANK, LANES), F32), struct((3, RANK, HEAD_SIZE), F32), struct((RANK, TOKENS), F32),
        ],
        in_specs=[SMEM] + [VMEM] * 13,
        out_specs=[VMEM] * 3,
        scratch_shapes=[pltpu.VMEM((3, LANES, TOKENS), BF16)],
        compiler_params=params(32),
        cost_estimate=cost(4),
        name="prior_dscore",
    )(ids, g, k, v, vm, qmt, qup, vup, kv_prior, vmt_prior, w, dvp, vb, dqm)


def shards(
    layer_input,
    frozen_queries,
    frozen_keys,
    frozen_values,
    output_gradient,
    norm_scale_vector,
    query_down_weight,
    query_up_weight,
    value_down_weight,
    value_up_weight,
    head_ordering,
):
    x, q, k, v, g = (
        a[0] for a in (layer_input, frozen_queries, frozen_keys, frozen_values, output_gradient)
    )
    ids, qup, vup = head_ordering, query_up_weight, value_up_weight
    scale = norm_scale_vector.reshape(1, WIDTH)
    down = jnp.concatenate(
        [query_down_weight, value_down_weight, jnp.broadcast_to(scale, (16, WIDTH))], axis=0
    )

    normed, qm, vm, qmt, vmt = pl.pallas_call(
        norm_kernel,
        out_shape=[
            struct((TOKENS, WIDTH), BF16), struct((TOKENS, RANK), BF16), struct((TOKENS, RANK), BF16),
            struct((RANK, TOKENS), BF16), struct((RANK, TOKENS), BF16),
        ],
        grid=(2,),
        in_specs=[pl.BlockSpec((HALF, WIDTH), lambda i: (i, 0)), whole((32, WIDTH))],
        out_specs=[
            pl.BlockSpec((HALF, WIDTH), lambda i: (i, 0)),
            pl.BlockSpec((HALF, RANK), lambda i: (i, 0)),
            pl.BlockSpec((HALF, RANK), lambda i: (i, 0)),
            pl.BlockSpec((RANK, HALF), lambda i: (0, i)),
            pl.BlockSpec((RANK, HALF), lambda i: (0, i)),
        ],
        compiler_params=params(20),
        cost_estimate=cost(5),
        name="norm",
    )(x, down)

    keys_out, values_out = pl.pallas_call(
        pick_kernel,
        out_shape=[struct((3, TOKENS, HEAD_SIZE), BF16), struct((4, TOKENS, HEAD_SIZE), BF16)],
        in_specs=[SMEM] + [VMEM] * 5,
        out_specs=[VMEM] * 2,
        compiler_params=params(8),
        name="pick",
    )(ids, k, v, vm, vmt, vup)
    keys_prior = from_behind(keys_out, 1)
    values_prior = from_behind(values_out, 1)

    qb1, vb1, dqm1, dvm1 = own_call(ids, q, g, k, v, qm, vm, qmt, vmt, qup, vup)
    w, dvp, vbp, dvm, handed = weights_call(ids, q, g, k, qm, vmt, qup, vup, keys_prior, dvm1)
    handed = from_behind(handed, -1)
    qb2, vb2, dqm = dscore_call(
        ids, g, k, v, vm, qmt, qup, vup, keys_prior, values_prior, w, dvp, vbp, dqm1
    )

    keep, send = pl.pallas_call(
        gather_kernel,
        out_shape=[struct((PART, 16, HEAD_SIZE), BF16)] * 2,
        in_specs=[SMEM] + [VMEM] * 8,
        out_specs=[VMEM] * 2,
        scratch_shapes=[
            pltpu.VMEM((2, PART, 16, HEAD_SIZE), BF16), pltpu.VMEM((32, 16, HEAD_SIZE), F32),
        ],
        compiler_params=params(16),
        name="gradients",
    )(ids, normed, dqm, dvm, handed, qb1, vb1, qb2, vb2)

    mine, other = sum_over_devices(keep, send)

    listed_items = RANK * (2 * WIDTH + KV_HEADS * LANES + KV_HEADS * HEAD_SIZE) + WIDTH
    qa, qb, va, vb, gain = pl.pallas_call(
        functools.partial(clip_kernel, math.sqrt(listed_items)),
        out_shape=[
            jax.ShapeDtypeStruct((RANK, WIDTH), F32),
            jax.ShapeDtypeStruct((RANK, KV_HEADS * LANES), F32),
            jax.ShapeDtypeStruct((RANK, WIDTH), F32),
            jax.ShapeDtypeStruct((RANK, KV_HEADS * HEAD_SIZE), F32),
            jax.ShapeDtypeStruct((1, WIDTH), F32),
        ],
        scratch_shapes=[pltpu.VMEM((1, WIDTH), F32), pltpu.VMEM((2, PART, 16, HEAD_SIZE), BF16)],
        compiler_params=params(16),
        name="clip",
    )(mine, other, query_down_weight, value_down_weight, scale)
    return (qa, qb, va, vb, gain.reshape(WIDTH))


def solution(mesh):
    placed = P("dp", "seq", None)
    return jax.shard_map(
        shards,
        mesh=mesh,
        in_specs=(placed,) * 5 + (P(),) * 6,
        out_specs=(P(), P(), P(), P(), P()),
        check_vma=False,
    )
```

```python
import functools
import math

import jax
import jax.numpy as jnp
from jax import lax
from jax.experimental import pallas as pl
from jax.experimental.pallas import tpu as pltpu
from jax.sharding import PartitionSpec as P

HEAD_SIZE = 128
TOKENS = 256
HALF = 128
WIDTH = 8192
RANK = 8
KV_HEADS = 6
SHARE = 8
LANES = SHARE * HEAD_SIZE
EPS = 1e-05
FACTOR = 1.0 / math.sqrt(HEAD_SIZE)
LOG2_E = 1.4426950408889634
TILES = 96
QB_TILE = 64
PART = TILES // 2
F32 = jnp.float32
BF16 = jnp.bfloat16
BOTH = ("seq", "dp")
MIB = 1024 * 1024


def nn(left, right):
    return jnp.dot(left, right, preferred_element_type=F32)


def nt(left, right):
    return lax.dot_general(left, right, (((1,), (1,)), ((), ())), preferred_element_type=F32)


def norm_kernel(x_ref, down_ref, normed_ref, qm_ref, vm_ref, qmt_ref, vmt_ref):
    step = 1024
    total = jnp.zeros((HALF, HEAD_SIZE), F32)
    for start in range(0, WIDTH, HEAD_SIZE):
        part = x_ref[:, start : start + HEAD_SIZE].astype(F32)
        total = total + part * part
    mean = jnp.sum(total, axis=1, keepdims=True) * (1.0 / WIDTH)
    inverse = lax.rsqrt(mean + EPS)
    mid = jnp.zeros((HALF, 2 * RANK), F32)
    for start in range(0, WIDTH, step):
        cols = slice(start, start + step)
        down = down_ref[:, cols]
        unit = x_ref[:, cols].astype(F32) * inverse
        normed = (unit * down[16:32].astype(F32)[:1]).astype(BF16)
        normed_ref[:, cols] = normed
        mid = mid + nt(normed, down[:16])
    qm_ref[...] = mid[:, :RANK].astype(BF16)
    vm_ref[...] = mid[:, RANK:].astype(BF16)
    mid_t = mid.T
    qmt_ref[...] = mid_t[:RANK].astype(BF16)
    vmt_ref[...] = mid_t[RANK:].astype(BF16)


def pick_kernel(ids_ref, k_ref, after_ref, keys_ref):
    for i in range(3):
        keys_ref[i] = k_ref[:, head_cols(ids_ref, 3 + i, HEAD_SIZE)]


def head_at(ids_ref, place):
    odd = lax.axis_index("seq") % 2
    return jnp.where(odd == 1, ids_ref[(place + 3) % KV_HEADS], ids_ref[place])


def head_cols(ids_ref, place, size):
    return pl.ds(pl.multiple_of(head_at(ids_ref, place) * size, size), size)


def token_rows(c):
    return slice(c * HALF, (c + 1) * HALF)


def share(part):
    return range(part * WIDE, (part + 1) * WIDE)


def stacked(ref, i, c, part):
    return jnp.concatenate(
        [ref[i, token_rows(c), j * HEAD_SIZE : (j + 1) * HEAD_SIZE] for j in share(part)], axis=0
    )


def stacked_grads(ref, ids_ref, place, c, part):
    start = head_at(ids_ref, place) * LANES
    return jnp.concatenate(
        [
            ref[token_rows(c), pl.ds(pl.multiple_of(start + j * HEAD_SIZE, HEAD_SIZE), HEAD_SIZE)]
            for j in share(part)
        ],
        axis=0,
    )


def causal_mask():
    key_id = lax.broadcasted_iota(jnp.int32, (HALF, HALF), 0)
    query_id = lax.broadcasted_iota(jnp.int32, (HALF, HALF), 1)
    return jnp.concatenate([key_id <= query_id] * WIDE, axis=1)


def transposed(array):
    return array.astype(F32).T.astype(BF16)


def adapted(frozen, mid, up):
    doubled = (2.0 * mid.astype(F32)).astype(BF16)
    return (frozen.astype(F32) + nn(doubled, up)).astype(BF16)


def own_scores(keys, queries, c, mask):
    own = nt(keys[: (c + 1) * HALF], queries) * (FACTOR * LOG2_E)
    if c == 0:
        return [jnp.where(mask, own, -jnp.inf)]
    return [own[:HALF], jnp.where(mask, own[HALF:], -jnp.inf)]


def softmax(parts):
    top = functools.reduce(jnp.maximum, [jnp.max(s, axis=0, keepdims=True) for s in parts])
    exps = [jnp.exp2(s - top) for s in parts]
    denom = functools.reduce(jnp.add, [jnp.sum(e, axis=0, keepdims=True) for e in exps])
    inv = 1.0 / denom
    return [e * inv for e in exps]


def summed_over_keys(parts):
    return functools.reduce(jnp.add, [jnp.sum(p, axis=0, keepdims=True) for p in parts])


def keep_dq(dq_scr, i, c, part, dq_t):
    dq_b = (dq_t * FACTOR).astype(BF16)
    for n, j in enumerate(share(part)):
        dq_scr[i, j * HEAD_SIZE : (j + 1) * HEAD_SIZE, token_rows(c)] = dq_b[:, n * HALF : (n + 1) * HALF]


def accumulate(totals, name, first, value):
    totals[name] = value if first else totals[name] + value


WIDE = 2
AHEAD = 4
UNITS = [(i, c, part) for i in range(3) for c in range(2) for part in range(SHARE // WIDE)]


def pipelined(before, after):
    states = [before(*unit) for unit in UNITS[:AHEAD]]
    for n, unit in enumerate(UNITS):
        if n + AHEAD < len(UNITS):
            states.append(before(*UNITS[n + AHEAD]))
        after(*unit, states.pop(0))


def own_kernel(
    ids_ref, q_ref, g_ref, k_ref, v_ref, qm_ref, vm_ref, qmt_ref, vmt_ref, qup_ref, vup_ref,
    qb_ref, vb_ref, dqm_ref, dvm_ref, values_ref, q_scr, dq_scr,
):
    mask = causal_mask()
    heads = {}
    totals = {}

    def before(i, c, part):
        if c == 0 and part == 0:
            small = head_cols(ids_ref, 3 + i, HEAD_SIZE)
            keys = k_ref[:, small]
            vup, qup = vup_ref[:, small], qup_ref[:, head_cols(ids_ref, 3 + i, LANES)]
            q_scr[i] = adapted(q_ref[:, head_cols(ids_ref, 3 + i, LANES)], qm_ref[...], qup)
            values = adapted(v_ref[:, small], vm_ref[...], vup)
            values_ref[i] = values
            heads[i] = (keys, transposed(keys), values, qup, vup)
        keys, _, values, _, _ = heads[i]
        grads = stacked_grads(g_ref, ids_ref, 3 + i, c, part)
        return own_scores(keys, stacked(q_scr, i, c, part), c, mask), nt(values[: (c + 1) * HALF], grads), grads

    def after(i, c, part, state):
        parts, dprob, grads = state
        _, keys_t, _, qup, vup = heads[i]
        probs = softmax(parts)
        dprobs = [dprob[j * HALF : (j + 1) * HALF] for j in range(c + 1)]
        weights = [p.astype(BF16) for p in probs]
        delta = summed_over_keys([w.astype(F32) * d for w, d in zip(weights, dprobs)])
        dscore = [(p * (d - delta)).astype(BF16) for p, d in zip(probs, dprobs)]
        near = (c + 1) * HALF
        keep_dq(dq_scr, i, c, part, nn(keys_t[:, :near], jnp.concatenate(dscore, axis=0)))
        term = nn(jnp.concatenate(weights, axis=0), grads)
        accumulate(totals, "low", c == 0 and part == 0, term[:HALF])
        if c == 0:
            return
        accumulate(totals, "high", part == 0, term[HALF:])
        if part < SHARE // WIDE - 1:
            return
        dv = jnp.concatenate([totals["low"], totals["high"]], axis=0).astype(BF16)
        dq_t = dq_scr[i]
        qb_ref[i] = 2.0 * nt(qmt_ref[...], dq_t)
        vb_ref[i] = 2.0 * nn(vmt_ref[...], dv)
        dq, dv = 2.0 * nn(qup, dq_t), 2.0 * nt(vup, dv)
        totals["dq"] = totals["dq"] + dq if i else dq
        totals["dv"] = totals["dv"] + dv if i else dv

    pipelined(before, after)
    dqm_ref[...] = totals["dq"]
    dvm_ref[...] = totals["dv"]
    mid_t = vmt_ref[...].astype(F32)
    pad = jnp.zeros((RANK, HEAD_SIZE), F32)
    values_ref[3] = jnp.zeros((TOKENS, HEAD_SIZE), BF16)
    for j in range(2):
        block = jnp.concatenate([mid_t[:, j * HEAD_SIZE : (j + 1) * HEAD_SIZE], pad], axis=0)
        values_ref[3, j * 16 : (j + 1) * 16] = block.astype(BF16)


def weights_kernel(
    ids_ref, q_ref, g_ref, k_ref, qm_ref, vmt_ref, qup_ref, vup_ref, kp_ref, dvm1_ref,
    w_ref, dvp_ref, vb_ref, dvm_ref, handed_ref, q_scr,
):
    mask = causal_mask()
    heads = {}
    totals = {"dv": dvm1_ref[...]}

    def before(i, c, part):
        if c == 0 and part == 0:
            small = head_cols(ids_ref, i, HEAD_SIZE)
            qup = qup_ref[:, head_cols(ids_ref, i, LANES)]
            q_scr[i] = adapted(q_ref[:, head_cols(ids_ref, i, LANES)], qm_ref[...], qup)
            heads[i] = (k_ref[:, small], kp_ref[i], vup_ref[:, small])
        keys, prior, _ = heads[i]
        queries = stacked(q_scr, i, c, part)
        return own_scores(keys, queries, c, mask), nt(prior, queries) * (FACTOR * LOG2_E)

    def after(i, c, part, state):
        own, prior = state
        probs = softmax(own + [prior])
        weights = jnp.concatenate([p.astype(BF16) for p in probs], axis=0)
        rows = 3 * HALF + c * HALF
        w_ref[i, c * 3 * HALF : c * 3 * HALF + rows, part * WIDE * HALF : (part + 1) * WIDE * HALF] = weights
        grads = stacked_grads(g_ref, ids_ref, i, c, part)
        term = nn(weights, grads)
        near = (c + 1) * HALF
        accumulate(totals, "low", c == 0 and part == 0, term[:HALF])
        accumulate(totals, "prior", c == 0 and part == 0, term[near:])
        if c == 0:
            return
        accumulate(totals, "high", part == 0, term[HALF:near])
        if part < SHARE // WIDE - 1:
            return
        dv = jnp.concatenate([totals["low"], totals["high"]], axis=0).astype(BF16)
        dv_prior = totals["prior"].astype(BF16)
        _, _, vup = heads[i]
        dvp_ref[i] = dv_prior
        vb_ref[i] = 2.0 * nn(vmt_ref[...], dv)
        totals["dv"] = totals["dv"] + 2.0 * nt(vup, dv)
        handed = 2.0 * nt(vup, dv_prior)
        totals["handed"] = totals["handed"] + handed if i else handed

    pipelined(before, after)
    dvm_ref[...] = totals["dv"]
    handed_ref[...] = totals["handed"]


def dscore_kernel(
    ids_ref, g_ref, k_ref, v_ref, vm_ref, qmt_ref, qup_ref, vup_ref, kp_ref, vp_ref,
    w_ref, dvp_ref, vb1_ref, dqm1_ref, qb_ref, vb_ref, dqm_ref, dq_scr,
):
    vmt_prior = jnp.concatenate(
        [vp_ref[3, j * 16 : (j + 1) * 16].astype(F32)[:RANK] for j in range(2)], axis=1
    ).astype(BF16)
    heads = {}
    totals = {"dq": dqm1_ref[...]}

    def before(i, c, part):
        if c == 0 and part == 0:
            small = head_cols(ids_ref, i, HEAD_SIZE)
            vup = vup_ref[:, small]
            heads[i] = (
                transposed(k_ref[:, small]),
                transposed(kp_ref[i]),
                adapted(v_ref[:, small], vm_ref[...], vup),
                vp_ref[i],
            )
        _, _, values, prior = heads[i]
        grads = stacked_grads(g_ref, ids_ref, i, c, part)
        return nt(values[: (c + 1) * HALF], grads), nt(prior, grads)

    def after(i, c, part, dprobs):
        keys_t, prior_t, _, _ = heads[i]
        near = (c + 1) * HALF
        start = c * 3 * HALF
        cols = slice(part * WIDE * HALF, (part + 1) * WIDE * HALF)
        weights = [
            w_ref[i, start : start + near, cols].astype(F32),
            w_ref[i, start + near : start + near + TOKENS, cols].astype(F32),
        ]
        delta = summed_over_keys([w * d for w, d in zip(weights, dprobs)])
        dscore = [(w * (d - delta)).astype(BF16) for w, d in zip(weights, dprobs)]
        keep_dq(dq_scr, i, c, part, nn(keys_t[:, :near], dscore[0]) + nn(prior_t, dscore[1]))
        if c == 0 or part < SHARE // WIDE - 1:
            return
        dq_t = dq_scr[i]
        qb_ref[i] = 2.0 * nt(qmt_ref[...], dq_t)
        vb_ref[i] = vb1_ref[i] + 2.0 * nn(vmt_prior, dvp_ref[i])
        totals["dq"] = totals["dq"] + 2.0 * nn(qup_ref[:, head_cols(ids_ref, i, LANES)], dq_t)

    pipelined(before, after)
    dqm_ref[...] = totals["dq"]


def gather_kernel(
    ids_ref, normed_ref, dqm_ref, dvm_ref, dvh_ref, qb1_ref, vb1_ref, qb2_ref, vb2_ref,
    keep_ref, send_ref, tiles, buf,
):
    mids = jnp.concatenate([dqm_ref[...], dvm_ref[...] + dvh_ref[...]], axis=0).astype(BF16)
    buf[27:32] = jnp.zeros((5, 16, HEAD_SIZE), F32)
    for i in range(3):
        for base, qb_ref, vb_ref in ((0, qb2_ref, vb2_ref), (3, qb1_ref, vb1_ref)):
            head = head_at(ids_ref, base + i)
            upper = head >= 3
            row = pl.multiple_of(jnp.where(upper, 8, 0), 8)
            place = jnp.where(upper, head - 3, head)
            for k in range(SHARE):
                buf[place * SHARE + k, pl.ds(row, 8), :] = qb_ref[i][:, k * HEAD_SIZE : (k + 1) * HEAD_SIZE]
            buf[24 + place, pl.ds(row, 8), :] = vb_ref[i]
    for j in range(16):
        part = nn(mids, normed_ref[:, j * 512 : (j + 1) * 512]).astype(BF16)
        for k in range(4):
            t = 4 * j + k
            tiles[t // PART, t % PART] = part[:, k * HEAD_SIZE : (k + 1) * HEAD_SIZE]
    for t in range(QB_TILE, TILES):
        tiles[t // PART, t % PART] = buf[t - QB_TILE].astype(BF16)
    core = lax.axis_index("dp") % 2
    keep_ref[...] = tiles[core]
    send_ref[...] = tiles[1 - core]


def clip_kernel(
    limit, mine_ref, other_ref, qd_ref, vd_ref, scale_ref,
    qa_ref, qb_ref, va_ref, vb_ref, gain_ref, gains, both,
):
    core = lax.axis_index("dp") % 2
    both[core] = mine_ref[...]
    both[1 - core] = other_ref[...]

    def summed(t):
        return both[t // PART, t % PART].astype(F32)

    total = jnp.zeros((16, HEAD_SIZE), F32)
    gain_total = jnp.zeros((1, HEAD_SIZE), F32)
    for t in range(QB_TILE):
        cols = slice(t * HEAD_SIZE, (t + 1) * HEAD_SIZE)
        tile = summed(t)
        total = total + tile * tile
        mixed = qd_ref[:, cols].astype(F32) * tile[:RANK] + vd_ref[:, cols].astype(F32) * tile[RANK:]
        gain = jnp.sum(mixed, axis=0, keepdims=True) / scale_ref[:, cols].astype(F32)
        gains[:, cols] = gain
        gain_total = gain_total + gain * gain
    for t in range(QB_TILE, QB_TILE + 27):
        tile = summed(t)
        total = total + tile * tile
    squares = jnp.sum(total, keepdims=True) + jnp.sum(gain_total, keepdims=True)
    factor = jnp.minimum(1.0, limit / jnp.sqrt(squares))
    gain_ref[...] = gains[...] * factor
    for t in range(QB_TILE):
        cols = slice(t * HEAD_SIZE, (t + 1) * HEAD_SIZE)
        tile = summed(t) * factor
        qa_ref[:, cols] = tile[:RANK]
        va_ref[:, cols] = tile[RANK:]
    for t in range(24):
        tile = summed(QB_TILE + t) * factor
        qb_ref[:, t * HEAD_SIZE : (t + 1) * HEAD_SIZE] = tile[:RANK]
        qb_ref[:, (24 + t) * HEAD_SIZE : (25 + t) * HEAD_SIZE] = tile[RANK:]
    for t in range(3):
        tile = summed(QB_TILE + 24 + t) * factor
        vb_ref[:, t * HEAD_SIZE : (t + 1) * HEAD_SIZE] = tile[:RANK]
        vb_ref[:, (3 + t) * HEAD_SIZE : (4 + t) * HEAD_SIZE] = tile[RANK:]


def groups_along(keys):
    found = {}
    for device in range(256):
        y, xh, z, rest = device // 64, device // 32 % 2, device // 4 % 8, device % 4
        place = {"y": y, "xh": xh, "z": z, "xl": rest // 2, "core": rest % 2}
        found.setdefault(tuple(v for k, v in place.items() if k not in keys), []).append(device)
    return list(found.values())


PLANE = groups_along(("y", "xh", "xl"))
COLUMN = groups_along(("z",))


def exchange(array, groups):
    return lax.all_to_all(array, BOTH, 0, 0, tiled=True, axis_index_groups=groups)


def other_core(array):
    return lax.ppermute(array, "dp", [(i, i ^ 1) for i in range(32)])


def sum_over_devices(keep, send):
    shares = (keep.astype(F32) + other_core(send).astype(F32)).astype(BF16)
    shares = shares.reshape(16, 3, 16, HEAD_SIZE)
    mine = jnp.sum(exchange(shares, PLANE).astype(F32), axis=0).astype(BF16)
    copies = jnp.broadcast_to(mine[None], (8, 3, 16, HEAD_SIZE))
    mine = jnp.sum(exchange(copies, COLUMN).astype(F32), axis=0).astype(BF16)
    copies = jnp.broadcast_to(mine[None], (16, 3, 16, HEAD_SIZE))
    whole_part = exchange(copies, PLANE).reshape(PART, 16, HEAD_SIZE)
    return whole_part, other_core(whole_part)


def from_behind(block, distance):
    return lax.ppermute(block, "seq", [((i - distance) % 8, i) for i in range(8)])


def whole(shape):
    return pl.BlockSpec(shape, lambda *_: (0,) * len(shape))


def params(mib):
    return pltpu.CompilerParams(vmem_limit_bytes=mib * MIB)


def struct(shape, dtype):
    return jax.ShapeDtypeStruct(shape, dtype)


VMEM = pl.BlockSpec(memory_space=pltpu.VMEM)
SMEM = pl.BlockSpec(memory_space=pltpu.SMEM)
HBM = pl.BlockSpec(memory_space=pl.ANY)


def cost(us):
    return pl.CostEstimate(flops=int(us * 1e9), bytes_accessed=0, transcendentals=0)


def own_call(ids, q, g, k, v, qm, vm, qmt, vmt, qup, vup):
    return pl.pallas_call(
        own_kernel,
        out_shape=[
            struct((3, RANK, LANES), F32), struct((3, RANK, HEAD_SIZE), F32),
            struct((RANK, TOKENS), F32), struct((RANK, TOKENS), F32), struct((4, TOKENS, HEAD_SIZE), BF16),
        ],
        in_specs=[SMEM] + [VMEM] * 10,
        out_specs=[VMEM] * 5,
        scratch_shapes=[pltpu.VMEM((3, TOKENS, LANES), BF16), pltpu.VMEM((3, LANES, TOKENS), BF16)],
        compiler_params=params(28),
        cost_estimate=cost(1),
        name="own_attention",
    )(ids, q, g, k, v, qm, vm, qmt, vmt, qup, vup)


def weights_call(ids, q, g, k, qm, vmt, qup, vup, kv_prior, dvm):
    return pl.pallas_call(
        weights_kernel,
        out_shape=[
            struct((3, 7 * HALF, LANES), BF16), struct((3, TOKENS, HEAD_SIZE), BF16),
            struct((3, RANK, HEAD_SIZE), F32), struct((RANK, TOKENS), F32), struct((RANK, TOKENS), F32),
        ],
        in_specs=[SMEM] + [VMEM] * 9,
        out_specs=[VMEM] * 5,
        scratch_shapes=[pltpu.VMEM((3, TOKENS, LANES), BF16)],
        compiler_params=params(32),
        cost_estimate=cost(4),
        name="prior_weights",
    )(ids, q, g, k, qm, vmt, qup, vup, kv_prior, dvm)


def dscore_call(ids, g, k, v, vm, qmt, qup, vup, kv_prior, vmt_prior, w, dvp, vb, dqm):
    return pl.pallas_call(
        dscore_kernel,
        out_shape=[
            struct((3, RANK, LANES), F32), struct((3, RANK, HEAD_SIZE), F32), struct((RANK, TOKENS), F32),
        ],
        in_specs=[SMEM] + [VMEM] * 13,
        out_specs=[VMEM] * 3,
        scratch_shapes=[pltpu.VMEM((3, LANES, TOKENS), BF16)],
        compiler_params=params(32),
        cost_estimate=cost(4),
        name="prior_dscore",
    )(ids, g, k, v, vm, qmt, qup, vup, kv_prior, vmt_prior, w, dvp, vb, dqm)


def shards(
    layer_input,
    frozen_queries,
    frozen_keys,
    frozen_values,
    output_gradient,
    norm_scale_vector,
    query_down_weight,
    query_up_weight,
    value_down_weight,
    value_up_weight,
    head_ordering,
):
    x, q, k, v, g = (
        a[0] for a in (layer_input, frozen_queries, frozen_keys, frozen_values, output_gradient)
    )
    ids, qup, vup = head_ordering, query_up_weight, value_up_weight
    scale = norm_scale_vector.reshape(1, WIDTH)
    down = jnp.concatenate(
        [query_down_weight, value_down_weight, jnp.broadcast_to(scale, (16, WIDTH))], axis=0
    )

    normed, qm, vm, qmt, vmt = pl.pallas_call(
        norm_kernel,
        out_shape=[
            struct((TOKENS, WIDTH), BF16), struct((TOKENS, RANK), BF16), struct((TOKENS, RANK), BF16),
            struct((RANK, TOKENS), BF16), struct((RANK, TOKENS), BF16),
        ],
        grid=(2,),
        in_specs=[pl.BlockSpec((HALF, WIDTH), lambda i: (i, 0)), whole((32, WIDTH))],
        out_specs=[
            pl.BlockSpec((HALF, WIDTH), lambda i: (i, 0)),
            pl.BlockSpec((HALF, RANK), lambda i: (i, 0)),
            pl.BlockSpec((HALF, RANK), lambda i: (i, 0)),
            pl.BlockSpec((RANK, HALF), lambda i: (0, i)),
            pl.BlockSpec((RANK, HALF), lambda i: (0, i)),
        ],
        compiler_params=params(20),
        cost_estimate=cost(5),
        name="norm",
    )(x, down)

    keys_out = pl.pallas_call(
        pick_kernel,
        out_shape=struct((3, TOKENS, HEAD_SIZE), BF16),
        in_specs=[SMEM] + [VMEM] * 2,
        out_specs=VMEM,
        compiler_params=params(8),
        name="pick",
    )(ids, k, vmt)
    keys_prior = from_behind(keys_out, 1)

    qb1, vb1, dqm1, dvm1, values_out = own_call(ids, q, g, k, v, qm, vm, qmt, vmt, qup, vup)
    values_prior = from_behind(values_out, 1)
    w, dvp, vbp, dvm, handed = weights_call(ids, q, g, k, qm, vmt, qup, vup, keys_prior, dvm1)
    handed = from_behind(handed, -1)
    qb2, vb2, dqm = dscore_call(
        ids, g, k, v, vm, qmt, qup, vup, keys_prior, values_prior, w, dvp, vbp, dqm1
    )

    keep, send = pl.pallas_call(
        gather_kernel,
        out_shape=[struct((PART, 16, HEAD_SIZE), BF16)] * 2,
        in_specs=[SMEM] + [VMEM] * 8,
        out_specs=[VMEM] * 2,
        scratch_shapes=[
            pltpu.VMEM((2, PART, 16, HEAD_SIZE), BF16), pltpu.VMEM((32, 16, HEAD_SIZE), F32),
        ],
        compiler_params=params(16),
        name="gradients",
    )(ids, normed, dqm, dvm, handed, qb1, vb1, qb2, vb2)

    mine, other = sum_over_devices(keep, send)

    listed_items = RANK * (2 * WIDTH + KV_HEADS * LANES + KV_HEADS * HEAD_SIZE) + WIDTH
    qa, qb, va, vb, gain = pl.pallas_call(
        functools.partial(clip_kernel, math.sqrt(listed_items)),
        out_shape=[
            jax.ShapeDtypeStruct((RANK, WIDTH), F32),
            jax.ShapeDtypeStruct((RANK, KV_HEADS * LANES), F32),
            jax.ShapeDtypeStruct((RANK, WIDTH), F32),
            jax.ShapeDtypeStruct((RANK, KV_HEADS * HEAD_SIZE), F32),
            jax.ShapeDtypeStruct((1, WIDTH), F32),
        ],
        scratch_shapes=[pltpu.VMEM((1, WIDTH), F32), pltpu.VMEM((2, PART, 16, HEAD_SIZE), BF16)],
        compiler_params=params(16),
        name="clip",
    )(mine, other, query_down_weight, value_down_weight, scale)
    return (qa, qb, va, vb, gain.reshape(WIDTH))


def solution(mesh):
    placed = P("dp", "seq", None)
    return jax.shard_map(
        shards,
        mesh=mesh,
        in_specs=(placed,) * 5 + (P(),) * 6,
        out_specs=(P(), P(), P(), P(), P()),
        check_vma=False,
    )
```
